32 devices in a mesh: gx: 4 (over x, core), gy: 8 (over z, y).
Axes of the slice: x: 2, y: 2, z: 4, core: 2. Of those that a mesh axis runs over, the one named last changes fastest.
Arguments:
- leaf_raw: float32 [4, 8, 768, 768], P('gx', 'gy'), may hold values from -32 to 80, as said below
- medium_class: int32 [4, 8, 12], P('gx', 'gy'), may hold values from 0 to 7
- wave_table: float32 [8], replicated, may hold values from 1 to 4
- boundary_data: float32 [4, 8, 384, 128], P('gx', 'gy'), may hold values from -6 to 6
Outputs:
- parent_rows: float32 [4, 8, 384, 1536], P('gx', 'gy')
- interface_values: float32 [4, 8, 384, 128], P('gx', 'gy')
The draws below stay inside these ranges and needn't reach their ends.
Inputs may be any that keep to these rules, and one draw needn't show every extreme that they name: Each tile's block leaf_raw[p, q] is symmetric positive semidefinite.
All inputs are finite; a program needn't handle non-finite values.
Results may differ from the reference program's by a relative error of at most 0.0001.
Values sent between devices are 32-bit elements; how exact they have to be, the bound alone decides.
No kernel may reach another device: no remote copies, remote signals or barrier semaphores. Data moves between devices by JAX's collectives and lax.ppermute only.
A program may use at most 64 MiB of HBM per device.

```python
import math
import jax
import jax.numpy as jnp
from jax import lax

SIDE = 192
BOUND = 768
NCOL = 128
BLK = 64
NBLK = 12
NCLS = 8
N_GX = 4
N_GY = 8


def side_kernel():
    amplitude = 24.0
    kernel_width = 8.0
    points = jnp.arange(BOUND, dtype=jnp.int32)
    side_index = points // SIDE
    along = (points % SIDE).astype(jnp.float32)
    distance = (along[:, None] - along[None, :]) / kernel_width
    same_side = (side_index[:, None] == side_index[None, :]).astype(jnp.float32)
    return amplitude * jnp.exp(-distance * distance) * same_side


def draw_leaf_raw(key, part):
    tile_count = N_GX * N_GY
    coupling = 16.0
    smooth_part = side_kernel()

    def one_tile(tile_index):
        tile_key = jax.random.fold_in(key, tile_index)
        factor_draw = jax.random.normal(tile_key, (BOUND, BOUND), jnp.float32)
        wishart = jnp.dot(factor_draw, factor_draw.T, precision=lax.Precision.HIGHEST, preferred_element_type=jnp.float32) * (coupling / BOUND)
        return wishart + smooth_part
    tile_maps = lax.map(one_tile, jnp.arange(tile_count, dtype=jnp.int32))
    return tile_maps.reshape(N_GX, N_GY, BOUND, BOUND)


def touch_ends(drawn, key, low, largest):
    extent = drawn.shape
    spot = [jax.random.randint(jax.random.fold_in(key, axis), (), 0, extent[axis]) for axis in range(len(extent))]
    drawn = drawn.at[tuple(spot)].set(low)
    longest = extent.index(max(extent))
    spot[longest] = (spot[longest] + 1) % extent[longest]
    return drawn.at[tuple(spot)].set(largest)


def level_of(stream_key, dims, cuts, smallest, largest):
    loudness, own = 1.0, jax.random.fold_in(stream_key, 6)
    for position, blocks in cuts:
        steps = jnp.exp(jax.random.uniform(jax.random.fold_in(own, position), (blocks,), jnp.float32, smallest / len(cuts), largest / len(cuts)))
        loudness = loudness * jnp.repeat(steps, dims[position] // blocks).reshape([-1 if axis == position else 1 for axis in range(len(dims))])
    return loudness


def noise(key, dims, spread, limit, shards=(), held_as=jnp.bfloat16):
    loudness = level_of(key, dims, shards, -0.22, 0.18) if shards else 1.0
    result = jax.random.normal(key, dims, jnp.float32) * spread * loudness
    return jnp.minimum(jnp.maximum(result, -limit), limit).astype(held_as)


def setup_inputs(seed: int = 0) -> dict:
    streams_of = jax.random.split(jax.random.key(seed), 5)
    leaf_raw = draw_leaf_raw(jax.random.fold_in(streams_of[4], 71), 0)
    medium_class = touch_ends(jax.random.randint(streams_of[1], (N_GX, N_GY, NBLK), 0, NCLS), jax.random.fold_in(streams_of[1], 1), 0, NCLS - 1).astype(jnp.int32)
    wave_table = jnp.clip(jnp.exp(jax.random.uniform(streams_of[2], (NCLS,), jnp.float32, math.log(1.0), math.log(4.0))), 1.0, 4.0)
    boundary_data = noise(streams_of[3], (N_GX, N_GY, 2 * SIDE, NCOL), 1.0, 6.0, ((0, 4), (1, 8)), jnp.float32)
    return {"leaf_raw": leaf_raw, "medium_class": medium_class, "wave_table": wave_table, "boundary_data": boundary_data}


highest = lax.Precision.HIGHEST

def product(left_mat, right_mat):
    return jnp.dot(left_mat.astype(jnp.float32), right_mat.astype(jnp.float32), precision=highest, preferred_element_type=jnp.float32)

def inner_product(left_mat, right_mat):
    return lax.dot_general(left_mat.astype(jnp.float32), right_mat.astype(jnp.float32), (((0,), (0,)), ((), ())), precision=highest, preferred_element_type=jnp.float32)

def lower_solve(factor, right_side):
    return lax.linalg.triangular_solve(factor, right_side, left_side=True, lower=True)

def upper_solve(factor, right_side):
    return lax.linalg.triangular_solve(factor, right_side, left_side=True, lower=True, transpose_a=True)

def level_outer(matrix, side_len):
    return jnp.concatenate([matrix[:, :2 * side_len], matrix[:, 3 * side_len:5 * side_len]], axis=1)

def level_inner(matrix, side_len):
    return jnp.concatenate([matrix[:, 2 * side_len:3 * side_len], matrix[:, 5 * side_len:]], axis=1)

def build_leaf(raw_block, classes, wave_table):
    diagonal = 4.0 + jnp.repeat(wave_table[classes], BLK)
    return 0.5 * (raw_block + raw_block.T) + jnp.diag(diagonal)

def merge_one(lower_leaf, upper_leaf):
    exterior = 3 * SIDE
    factor = jnp.linalg.cholesky(lower_leaf[exterior:, exterior:] + upper_leaf[exterior:, exterior:])
    solved = lower_solve(factor, jnp.concatenate([lower_leaf[exterior:, :exterior], upper_leaf[exterior:, :exterior]], axis=1))
    zero_block = jnp.zeros((exterior, exterior), jnp.float32)
    blocks = jnp.concatenate([jnp.concatenate([lower_leaf[:exterior, :exterior], zero_block], axis=1), jnp.concatenate([zero_block, upper_leaf[:exterior, :exterior]], axis=1)], axis=0)
    return (blocks - inner_product(solved, solved), factor, solved)

def rows_inner(matrix):
    return jnp.concatenate([matrix[2 * SIDE:3 * SIDE], matrix[5 * SIDE:]], axis=0)

def rows_outer(matrix):
    return jnp.concatenate([matrix[:2 * SIDE], matrix[3 * SIDE:5 * SIDE]], axis=0)

def merge_two(lower_parent, upper_parent):
    face_lower = rows_inner(lower_parent)
    face_upper = rows_inner(upper_parent)
    factor = jnp.linalg.cholesky(level_inner(face_lower, SIDE) + level_inner(face_upper, SIDE))
    solved = lower_solve(factor, jnp.concatenate([level_outer(face_lower, SIDE), level_outer(face_upper, SIDE)], axis=1))
    zero_block = jnp.zeros((4 * SIDE, 4 * SIDE), jnp.float32)
    blocks = jnp.concatenate([jnp.concatenate([level_outer(rows_outer(lower_parent), SIDE), zero_block], axis=1), jnp.concatenate([zero_block, level_outer(rows_outer(upper_parent), SIDE)], axis=1)], axis=0)
    return (blocks - inner_product(solved, solved), factor, solved)

def group_work(tiles_raw, tiles_class, wave_table, tiles_data):
    parents = []
    factors = []
    solveds = []
    for row_half in range(2):
        lower_leaf = build_leaf(tiles_raw[0, row_half], tiles_class[0, row_half], wave_table)
        upper_leaf = build_leaf(tiles_raw[1, row_half], tiles_class[1, row_half], wave_table)
        parent, factor, solved = merge_one(lower_leaf, upper_leaf)
        parents.append(parent)
        factors.append(factor)
        solveds.append(solved)
    top_map, factor_two, solved_two = merge_two(parents[0], parents[1])
    rows_four = jnp.swapaxes(top_map.reshape(2, 2, 2 * SIDE, 8 * SIDE), 0, 1)
    stacked = jnp.concatenate([tiles_data[0, 0], tiles_data[1, 0], tiles_data[0, 1], tiles_data[1, 1]], axis=0)
    gy_values = -upper_solve(factor_two, product(solved_two, stacked))
    columns = []
    for row_half in range(2):
        first_part = jnp.concatenate([tiles_data[0, row_half], gy_values[:SIDE]], axis=0)
        second_part = jnp.concatenate([tiles_data[1, row_half], gy_values[SIDE:]], axis=0)
        gx_values = -upper_solve(factors[row_half], product(solveds[row_half], jnp.concatenate([first_part, second_part], axis=0)))
        columns.append(jnp.stack([jnp.concatenate([gy_values[:SIDE], gx_values], axis=0), jnp.concatenate([gy_values[SIDE:], gx_values], axis=0)], axis=0))
    values_four = jnp.stack(columns, axis=1)
    return (rows_four, values_four)

def take_group(array, first_row, second_row):
    half_x = N_GX // 2
    half_y = N_GY // 2
    rest = array.shape[2:]
    anchor = tuple((jnp.int32(0) for _ in rest))
    outer_list = []
    for kx in range(2):
        inner_list = []
        for ky in range(2):
            start = (jnp.int32(first_row + kx * half_x), jnp.int32(second_row + ky * half_y)) + anchor
            inner_list.append(lax.dynamic_slice(array, start, (1, 1) + rest)[0, 0])
        outer_list.append(jnp.stack(inner_list, axis=0))
    return jnp.stack(outer_list, axis=0)

def put_group(array, group_vals, first_row, second_row):
    half_x = N_GX // 2
    half_y = N_GY // 2
    anchor = tuple((jnp.int32(0) for _ in array.shape[2:]))
    for kx in range(2):
        for ky in range(2):
            start = (jnp.int32(first_row + kx * half_x), jnp.int32(second_row + ky * half_y)) + anchor
            array = lax.dynamic_update_slice(array, group_vals[kx, ky][None, None], start)
    return array

def reference(leaf_raw, medium_class, wave_table, boundary_data):
    half_x = N_GX // 2
    half_y = N_GY // 2
    groups = half_x * half_y

    def group_step(group_index, state_pair):
        rows_all, values_all = state_pair
        group_index = jnp.asarray(group_index).astype(jnp.int32)
        first_row = (group_index // half_y).astype(jnp.int32)
        second_row = (group_index % half_y).astype(jnp.int32)
        tiles_raw = take_group(leaf_raw, first_row, second_row)
        tiles_class = take_group(medium_class, first_row, second_row)
        tiles_data = take_group(boundary_data, first_row, second_row)
        rows_four, values_four = group_work(tiles_raw, tiles_class, wave_table, tiles_data)
        rows_all = put_group(rows_all, rows_four, first_row, second_row)
        values_all = put_group(values_all, values_four, first_row, second_row)
        return (rows_all, values_all)
    start_state = (jnp.zeros((N_GX, N_GY, 2 * SIDE, 8 * SIDE), jnp.float32), jnp.zeros((N_GX, N_GY, 2 * SIDE, NCOL), jnp.float32))
    parent_rows, interface_values = lax.fori_loop(0, groups, group_step, start_state)
    return (parent_rows, interface_values)
```

```python
import functools

import jax
import jax.numpy as jnp
from jax import lax
from jax.experimental import pallas as pl
from jax.experimental.pallas import tpu as pltpu
from jax.sharding import PartitionSpec as P

f32 = jnp.float32
bf16 = jnp.bfloat16
VM = pl.BlockSpec(memory_space=pltpu.VMEM)
SM = pl.BlockSpec(memory_space=pltpu.SMEM)
LEAST = 4.0


def shifted(shard, axis):
    size = lax.axis_size(axis)
    return lax.ppermute(shard, axis, [(i, (i + size // 2) % size) for i in range(size)])


def parts_of(x, count=2):
    parts = []
    for _ in range(count - 1):
        parts.append(x.astype(bf16))
        x = x - parts[-1].astype(f32)
    return parts + [x.astype(bf16)]


def dot_of(left, right, contract):
    return lax.dot_general(left, right, (contract, ((), ())), preferred_element_type=f32)


def mul_parts(left, right, contract=((1,), (0,))):
    depth = max(len(left), len(right))
    total = None
    for order in reversed(range(depth)):
        for i in range(order + 1):
            if i < len(left) and order - i < len(right):
                term = dot_of(left[i], right[order - i], contract)
                total = term if total is None else total + term
    return total


def mul(left, right):
    return mul_parts(parts_of(left), parts_of(right))


def mul_t(left, right):
    return mul_parts(parts_of(left), parts_of(right), ((0,), (0,)))


def rows_of(shape):
    return lax.broadcasted_iota(jnp.int32, shape, 0)


def cols_of(shape):
    return lax.broadcasted_iota(jnp.int32, shape, 1)


def eye(n):
    return (rows_of((n, n)) == cols_of((n, n))).astype(f32)


def invert(mat_ref, least, inv_ref, res_ref):
    n = mat_ref.shape[0]
    unit = eye(n)
    mat = mat_ref[...]
    most = jnp.max(jnp.sum(jnp.abs(mat), axis=0, keepdims=True))
    scale = 2.0 / (most + least)
    eps = (most - least) / (most + least)
    res = unit - scale * mat
    gain = 2.0 / (2.0 - eps * eps)
    inv_ref[...] = (gain * scale) * (unit + res)
    res_parts = parts_of(res)
    res_ref[...] = (1.0 - gain) * unit + gain * mul_parts(res_parts, res_parts)

    def fast(carry):
        eps, noise = carry
        gain = 2.0 / (2.0 - eps * eps)
        inv = inv_ref[...]
        res_parts = parts_of(res_ref[...])
        inv_ref[...] = gain * (inv + mul_parts(res_parts, parts_of(inv)))
        res_ref[...] = (1.0 - gain) * unit + gain * mul_parts(res_parts, res_parts)
        return gain * eps * eps * 0.5, 2.0 * gain * eps * noise + 3e-5

    eps, noise = lax.while_loop(
        lambda carry: carry[0] > 0.02, fast, (gain * eps * eps * 0.5, jnp.float32(6e-5))
    )
    mat_parts = parts_of(mat, 3)

    def correct(bound):
        inv = inv_ref[...]
        inv_parts = parts_of(inv, 3)
        res = unit - mul_parts(mat_parts, inv_parts)
        inv_ref[...] = inv + mul_parts(inv_parts[:2], parts_of(res))
        return bound * bound

    lax.while_loop(
        lambda bound: bound > 1e-6,
        correct,
        jnp.minimum(eps + noise + 1e-5 * (most / least), 0.5),
    )


def pack_kernel(class_ref, table_ref, raw_ref, data_ref, one_ref, two_ref, three_ref, rest_ref):
    bound = raw_ref.shape[0]
    side = bound // 4
    blk = bound // class_ref.shape[0]
    shape = (side, side)
    row, col = rows_of(shape), cols_of(shape)

    def with_diagonal(face, start):
        level = jnp.zeros(shape, f32)
        for k in range(side // blk):
            value = LEAST + table_ref[class_ref[start // blk + k]]
            level = jnp.where(row // blk == k, value, level)
        return face + jnp.where(row == col, level, 0.0)

    face = with_diagonal(raw_ref[2 * side : 3 * side, 2 * side : 3 * side], 2 * side)
    inner = with_diagonal(raw_ref[3 * side :, 3 * side :], 3 * side)
    one_ref[:side, :side] = jnp.where(row <= col, inner, face)
    one_ref[:side, side:] = raw_ref[3 * side :, 2 * side : 3 * side]
    one_ref[side:, :] = jnp.zeros((8, 2 * side), f32)
    one_ref[side : side + 1, :side] = jnp.sum(
        jnp.where(row == col, face, 0.0), axis=0, keepdims=True
    )
    inner_out = raw_ref[3 * side :, : 2 * side]
    face_out = raw_ref[2 * side : 3 * side, : 2 * side]
    two_ref[...] = inner_out
    three_ref[...] = face_out
    rest_ref[:side] = inner_out
    rest_ref[side : 2 * side] = face_out
    ncol = data_ref.shape[1]
    for k in range(2 * side // ncol):
        rest_ref[2 * side :, k * ncol : (k + 1) * ncol] = data_ref[k * ncol : (k + 1) * ncol]


def unpack(one_ref):
    side = one_ref.shape[1] // 2
    shape = (side, side)
    row, col = rows_of(shape), cols_of(shape)
    packed = one_ref[:side, :side]
    flipped = packed.T
    inner = jnp.where(row <= col, packed, flipped)
    face = jnp.where(row > col, packed, jnp.where(row < col, flipped, one_ref[side : side + 1, :side]))
    return inner, face, one_ref[:side, side:]


def pair_level(least, own_ref, sib_ref, mat, res, inv_ref, fold_ref):
    side = own_ref.shape[1] // 2
    inner_a, face_a, cross_a = unpack(own_ref)
    inner_b, face_b, cross_b = unpack(sib_ref)
    mat[...] = inner_a + inner_b
    invert(mat, least, inv_ref, res)
    inv_parts = parts_of(inv_ref[...])
    parts_a, parts_b = parts_of(cross_a), parts_of(cross_b)
    fold_a = mul_parts(parts_a, inv_parts, ((0,), (0,)))
    fold_b = mul_parts(parts_b, inv_parts, ((0,), (0,)))
    fold_ref[:side] = fold_a
    fold_ref[side:] = fold_b
    fold_a, fold_b = parts_of(fold_a), parts_of(fold_b)
    aa = face_a - mul_parts(fold_a, parts_a)
    ab = -mul_parts(fold_a, parts_b)
    ba = -mul_parts(fold_b, parts_a)
    bb = face_b - mul_parts(fold_b, parts_b)
    return aa, ab, ba, bb


def least_of(table_ref):
    least = table_ref[0]
    for k in range(1, table_ref.shape[0]):
        least = jnp.minimum(least, table_ref[k])
    return 2.0 * (LEAST + least)


def own_kernel(table_ref, own_ref, sib_ref, inv_ref, fold_ref, face_ref, mat, res):
    side = own_ref.shape[1] // 2
    aa, ab, ba, bb = pair_level(least_of(table_ref), own_ref, sib_ref, mat, res, inv_ref, fold_ref)
    face_ref[:side, :side] = aa
    face_ref[:side, side:] = ab
    face_ref[side:, :side] = ba
    face_ref[side:, side:] = bb


def far_kernel(table_ref, own_ref, sib_ref, near_ref, fold_ref, inv2_ref, mat, res, inv, mat2, res2):
    side = own_ref.shape[1] // 2
    least = least_of(table_ref)
    aa, ab, ba, bb = pair_level(least, own_ref, sib_ref, mat, res, inv, fold_ref)
    mat2[:side, :side] = near_ref[:side, :side] + aa
    mat2[:side, side:] = near_ref[:side, side:] + ab
    mat2[side:, :side] = near_ref[side:, :side] + ba
    mat2[side:, side:] = near_ref[side:, side:] + bb
    invert(mat2, least, inv2_ref, res2)


def rows_kernel(inv_ref, fold_ref, rest_a, rest_b, own_ref, sib_ref, rows_a, rows_b, term_ref, known_ref):
    side = inv_ref.shape[0]
    ncol = term_ref.shape[1]
    fold = parts_of(fold_ref[...])
    term = known = None
    for rest, out, top in ((rest_a, rows_a, 0), (rest_b, rows_b, side)):
        inner_out = parts_of(rest[:side])
        out[...] = -mul_parts(fold, inner_out)
        out[top : top + side] += rest[side : 2 * side]
        data = parts_of(
            jnp.concatenate(
                [rest[2 * side :, k * ncol : (k + 1) * ncol] for k in range(2 * side // ncol)], axis=0
            )
        )
        add = mul_parts(parts_of(out[...]), data)
        more = mul_parts(inner_out, data)
        term = add if term is None else term + add
        known = more if known is None else known + more
    term_ref[...] = term
    known_ref[...] = known


def near_kernel(
    class_ref, table_ref, raw_ref, rest_a, rest_b, inv_ref, inv2_ref, rows_a, rows_b,
    out_a, out_b, scaled_ref,
):
    side = inv_ref.shape[0]
    blk = side * 4 // class_ref.shape[0]
    scaled = mul_t(rows_a[...], inv2_ref[...])
    scaled_ref[...] = scaled
    inner_a = parts_of(rest_a[:side])
    fold = parts_of(mul_parts(inner_a, parts_of(inv_ref[...]), ((0,), (0,))))
    scaled = parts_of(scaled)
    shape = (2 * side, 2 * side)
    row, col = rows_of(shape), cols_of(shape)
    level = jnp.zeros(shape, f32)
    for k in range(2 * side // blk):
        level = jnp.where(row // blk == k, LEAST + table_ref[class_ref[k]], level)
    outer = raw_ref[: 2 * side, : 2 * side] + jnp.where(row == col, level, 0.0)
    out_a[...] = outer - mul_parts(fold, inner_a) - mul_parts(scaled, parts_of(rows_a[...]))
    out_b[...] = -mul_parts(fold, parts_of(rest_b[:side])) - mul_parts(scaled, parts_of(rows_b[...]))


def last_kernel(place_ref, out_a, out_b, scaled_ref, fold_ref, two_c, two_d, three_c, three_d, out_ref):
    side = two_c.shape[0]
    width = 2 * side

    def put(k, value):
        out_ref[:, pl.ds(pl.multiple_of(place_ref[k] * width, width), width)] = value

    put(0, out_a[...])
    put(1, out_b[...])
    scaled = parts_of(scaled_ref[...])
    fold = parts_of(mul_parts(scaled, parts_of(fold_ref[...])))
    for k, two, three, top in ((2, two_c, three_c, 0), (3, two_d, three_d, side)):
        left = [part[:, top : top + side] for part in scaled]
        put(k, mul_parts(fold, parts_of(two[...])) - mul_parts(left, parts_of(three[...])))


def values_kernel(term_ref, half_ref, other_ref, known_ref, inv_ref, inv2_ref, own_ref, sib_ref, out_ref):
    side = inv_ref.shape[0]
    total = jnp.concatenate(
        [term_ref[:side] + half_ref[...], term_ref[side:] + other_ref[...]], axis=0
    )
    face = -mul(inv2_ref[...], total)
    out_ref[:side] = face[:side]
    inner = (
        known_ref[...]
        + mul(own_ref[:side, side:], face[:side])
        + mul(sib_ref[:side, side:], face[side:])
    )
    out_ref[side:] = -mul(inv_ref[...], inner)


def call(kernel, outs, args, specs=None, scratch=(), name=None, flops=0):
    return pl.pallas_call(
        kernel,
        out_shape=[jax.ShapeDtypeStruct(s, f32) for s in outs],
        in_specs=specs or [VM] * len(args),
        out_specs=[VM] * len(outs),
        scratch_shapes=[pltpu.VMEM(s, f32) for s in scratch],
        compiler_params=pltpu.CompilerParams(vmem_limit_bytes=48 * 1024 * 1024),
        cost_estimate=pl.CostEstimate(flops=flops, bytes_accessed=0, transcendentals=0),
        name=name,
    )(*args)


def body(leaf_raw, medium_class, wave_table, boundary_data):
    raw = leaf_raw[0, 0]
    classes = medium_class[0, 0]
    data = boundary_data[0, 0]
    bound = raw.shape[0]
    side = bound // 4
    ncol = data.shape[1]
    half_x = lax.axis_size("gx") // 2
    half_y = lax.axis_size("gy") // 2
    column = lax.axis_index("gx") // half_x
    row = lax.axis_index("gy") // half_y
    place = jnp.stack(
        [2 * row + column, 2 * row + 1 - column, 2 - 2 * row + column, 3 - 2 * row - column]
    ).astype(jnp.int32)

    one, two, three, rest = call(
        pack_kernel,
        [(side + 8, 2 * side), (side, 2 * side), (side, 2 * side), (2 * side + ncol, 2 * side)],
        (classes, wave_table, raw, data),
        [SM, SM, VM, VM],
        name="pack",
    )
    one_x = shifted(one, "gx")
    one_z = shifted(one, "gy")
    rest_x = shifted(rest, "gx")
    two_z = shifted(two, "gy")
    three_z = shifted(three, "gy")
    one_zx = shifted(one_z, "gx")
    two_zx = shifted(two_z, "gx")
    three_zx = shifted(three_z, "gx")

    sq, sq2 = (side, side), (2 * side, 2 * side)
    inv1, fold1, face1 = call(
        own_kernel, [sq, (2 * side, side), sq2], (wave_table, one, one_x), [SM, VM, VM], [sq, sq], "own_level"
    )
    rows_a, rows_b, term, known = call(
        rows_kernel,
        [sq2, sq2, (2 * side, ncol), (side, ncol)],
        (inv1, fold1, rest, rest_x, one, one_x),
        name="pair_rows",
    )
    half_z = shifted(term[:side], "gy")
    half_zx = shifted(half_z, "gx")
    fold2, inv2 = call(
        far_kernel,
        [(2 * side, side), sq2],
        (wave_table, one_z, one_zx, face1),
        [SM, VM, VM, VM],
        [sq, sq, sq, sq2, sq2],
        "far_level",
    )
    out_a, out_b, scaled = call(
        near_kernel,
        [sq2, sq2, sq2],
        (classes, wave_table, raw, rest, rest_x, inv1, inv2, rows_a, rows_b),
        [SM, SM] + [VM] * 7,
        name="near_rows",
    )
    (values,) = call(
        values_kernel,
        [(2 * side, ncol)],
        (term, half_z, half_zx, known, inv1, inv2, one, one_x),
        name="values",
    )
    (parent,) = call(
        last_kernel,
        [(2 * side, 8 * side)],
        (place, out_a, out_b, scaled, fold2, two_z, two_zx, three_z, three_zx),
        [SM] + [VM] * 8,
        name="far_rows",
    )
    return (parent[None, None], values[None, None])


def solution(mesh):
    return jax.shard_map(
        body,
        mesh=mesh,
        in_specs=(P("gx", "gy", None, None), P("gx", "gy", None), P(), P("gx", "gy", None, None)),
        out_specs=(P("gx", "gy", None, None), P("gx", "gy", None, None)),
        check_vma=False,
    )
```

```python
import functools

import jax
import jax.numpy as jnp
from jax import lax
from jax.experimental import pallas as pl
from jax.experimental.pallas import tpu as pltpu
from jax.sharding import PartitionSpec as P

f32 = jnp.float32
bf16 = jnp.bfloat16
VM = pl.BlockSpec(memory_space=pltpu.VMEM)
ANY = pl.BlockSpec(memory_space=pl.ANY)
HBM = pl.BlockSpec(memory_space=pltpu.HBM)
SM = pl.BlockSpec(memory_space=pltpu.SMEM)
LEAST = 4.0


def shifted(shard, axis):
    size = lax.axis_size(axis)
    return lax.ppermute(shard, axis, [(i, (i + size // 2) % size) for i in range(size)])


def parts_of(x, count=2):
    parts = []
    for _ in range(count - 1):
        parts.append(x.astype(bf16))
        x = x - parts[-1].astype(f32)
    return parts + [x.astype(bf16)]


def dot_of(left, right, contract):
    return lax.dot_general(left, right, (contract, ((), ())), preferred_element_type=f32)


def mul_parts(left, right, contract=((1,), (0,))):
    depth = max(len(left), len(right))
    total = None
    for order in reversed(range(depth)):
        for i in range(order + 1):
            if i < len(left) and order - i < len(right):
                term = dot_of(left[i], right[order - i], contract)
                total = term if total is None else total + term
    return total


def mul(left, right):
    return mul_parts(parts_of(left), parts_of(right))


def mul_t(left, right):
    return mul_parts(parts_of(left), parts_of(right), ((0,), (0,)))


def rows_of(shape):
    return lax.broadcasted_iota(jnp.int32, shape, 0)


def cols_of(shape):
    return lax.broadcasted_iota(jnp.int32, shape, 1)


def eye(n):
    return (rows_of((n, n)) == cols_of((n, n))).astype(f32)


def invert_start(mat, least, inv_ref, res_ref):
    n = mat.shape[0]
    unit = eye(n)
    most = jnp.max(jnp.sum(jnp.abs(mat), axis=0, keepdims=True))
    scale = 2.0 / (most + least)
    eps = (most - least) / (most + least)
    res = unit - scale * mat
    gain = 2.0 / (2.0 - eps * eps)
    inv_ref[...] = (gain * scale) * (unit + res)
    res_parts = parts_of(res)
    res_ref[...] = (1.0 - gain) * unit + gain * mul_parts(res_parts, res_parts)

    def fast(carry):
        eps, noise = carry
        gain = 2.0 / (2.0 - eps * eps)
        inv = inv_ref[...]
        high, low = parts_of(res_ref[...])
        inv_high, inv_low = parts_of(inv)
        if n > 256:
            right_high = jnp.concatenate([high, inv_high], axis=1)
            right_low = jnp.concatenate([low, inv_low], axis=1)
            both = dot_of(
                jnp.concatenate([high, high, low], axis=1),
                jnp.concatenate([right_high, right_low, right_high], axis=0),
                ((1,), (0,)),
            )
            square, step = both[:, :n], both[:, n:]
        else:
            square = mul_parts([high, low], [high, low])
            step = mul_parts([high, low], [inv_high, inv_low])
        inv_ref[...] = gain * (inv + step)
        res_ref[...] = (1.0 - gain) * unit + gain * square
        return gain * eps * eps * 0.5, 2.0 * gain * eps * noise + 3e-5

    eps, noise = lax.while_loop(
        lambda carry: carry[0] > 0.02, fast, (gain * eps * eps * 0.5, jnp.float32(6e-5))
    )
    return jnp.minimum(eps + noise + 1e-5 * (most / least), 0.5)


def invert_end(mat, bound, inv_ref):
    unit = eye(mat.shape[0])
    mat_parts = parts_of(mat, 3)

    def residual(inv_parts):
        return unit - mul_parts(mat_parts, inv_parts)

    def correct(bound):
        inv = inv_ref[...]
        inv_parts = parts_of(inv, 3)
        inv_ref[...] = inv + mul_parts(inv_parts[:2], parts_of(residual(inv_parts)))
        return bound * bound

    lax.while_loop(lambda bound: bound > 0.01, correct, bound)
    inv = inv_ref[...]
    inv_parts = parts_of(inv, 3)
    res_parts = parts_of(residual(inv_parts))
    step = mul_parts(inv_parts[:2], res_parts)
    inv_ref[...] = inv + (step + dot_of(step.astype(bf16), res_parts[0], ((1,), (0,))))


def invert(mat, least, inv_ref, res_ref):
    invert_end(mat, invert_start(mat, least, inv_ref, res_ref), inv_ref)


def pack_kernel(
    class_any, table_any, raw_any, data_any, one_ref, two_ref, three_ref, more_ref,
    classes, table, raw, data, sems,
):
    bound = raw_any.shape[0]
    side = bound // 4
    blk = bound // class_any.shape[0]
    shape = (side, side)
    copies = [
        pltpu.make_async_copy(class_any, classes, sems.at[0]),
        pltpu.make_async_copy(table_any, table, sems.at[1]),
        pltpu.make_async_copy(raw_any.at[pl.ds(2 * side, 2 * side)], raw, sems.at[2]),
        pltpu.make_async_copy(data_any, data, sems.at[3]),
    ]
    for copy in copies:
        copy.start()
    row, col = rows_of(shape), cols_of(shape)
    for copy in copies:
        copy.wait()
    least = table[0]
    for k in range(1, table.shape[0]):
        least = jnp.minimum(least, table[k])

    def level_of(index, start, count):
        level = jnp.zeros(index.shape, f32)
        for k in range(count):
            level = jnp.where(index // blk == k, LEAST + table[classes[start + k]], level)
        return level

    def with_diagonal(block, start):
        return block + jnp.where(row == col, level_of(row, start // blk, side // blk), 0.0)

    face = with_diagonal(raw[:side, 2 * side : 3 * side], 2 * side)
    inner = with_diagonal(raw[side:, 3 * side :], 3 * side)
    one_ref[:side, :side] = jnp.where(row <= col, inner, face)
    one_ref[:side, side:] = raw[side:, 2 * side : 3 * side]
    one_ref[side : side + 8, :] = jnp.zeros((8, 2 * side), f32)
    one_ref[side : side + 1, :side] = jnp.sum(
        jnp.where(row == col, face, 0.0), axis=0, keepdims=True
    )
    one_ref[side + 1 : side + 2, :] = level_of(cols_of((1, 2 * side)), 0, 2 * side // blk)
    one_ref[side + 2 : side + 3, :] = jnp.zeros((1, 2 * side), f32) + 2.0 * (LEAST + least)
    inner_out = raw[side:, : 2 * side]
    two_ref[...] = inner_out
    three_ref[...] = raw[:side, : 2 * side]
    more_ref[:side] = inner_out
    known = mul(inner_out, data[...])
    rows, ncol = more_ref.shape[0] - side, data.shape[1]
    for k in range(side // rows):
        more_ref[side:, k * ncol : (k + 1) * ncol] = known[k * rows : (k + 1) * rows]


def unpack(one_ref):
    side = one_ref.shape[1] // 2
    shape = (side, side)
    row, col = rows_of(shape), cols_of(shape)
    packed = one_ref[:side, :side]
    flipped = packed.T
    inner = jnp.where(row <= col, packed, flipped)
    face = jnp.where(row > col, packed, jnp.where(row < col, flipped, one_ref[side : side + 1, :side]))
    return inner, face, one_ref[:side, side:]


def least_of(one_ref):
    side = one_ref.shape[1] // 2
    return jnp.min(one_ref[side + 2 : side + 3, :])


def pair_level(own_ref, sib_ref, res, inv_ref, fold_ref):
    side = own_ref.shape[1] // 2
    inner_a, face_a, cross_a = unpack(own_ref)
    inner_b, face_b, cross_b = unpack(sib_ref)
    invert(inner_a + inner_b, least_of(own_ref), inv_ref, res)
    inv_parts = parts_of(inv_ref[...])
    parts_a, parts_b = parts_of(cross_a), parts_of(cross_b)
    fold_a = mul_parts(parts_a, inv_parts, ((0,), (0,)))
    fold_b = mul_parts(parts_b, inv_parts, ((0,), (0,)))
    fold_ref[:side] = fold_a
    fold_ref[side:] = fold_b
    fold_a, fold_b = parts_of(fold_a), parts_of(fold_b)
    aa = face_a - mul_parts(fold_a, parts_a)
    ab = -mul_parts(fold_a, parts_b)
    ba = -mul_parts(fold_b, parts_a)
    bb = face_b - mul_parts(fold_b, parts_b)
    return aa, ab, ba, bb


def own_kernel(own_ref, sib_ref, inv_ref, fold_ref, face_ref, res):
    side = own_ref.shape[1] // 2
    aa, ab, ba, bb = pair_level(own_ref, sib_ref, res, inv_ref, fold_ref)
    face_ref[:side, :side] = aa
    face_ref[:side, side:] = ab
    face_ref[side:, :side] = ba
    face_ref[side:, side:] = bb


def far_kernel(own_ref, sib_ref, near_ref, fold_ref, sum_ref, res, inv):
    side = own_ref.shape[1] // 2
    aa, ab, ba, bb = pair_level(own_ref, sib_ref, res, inv, fold_ref)
    sum_ref[:side, :side] = near_ref[:side, :side] + aa
    sum_ref[:side, side:] = near_ref[:side, side:] + ab
    sum_ref[side:, :side] = near_ref[side:, :side] + ba
    sum_ref[side:, side:] = near_ref[side:, side:] + bb


def face_start_kernel(own_ref, sum_ref, inv_ref, bound_ref, res):
    bound = invert_start(sum_ref[...], least_of(own_ref), inv_ref, res)
    bound_ref[...] = jnp.zeros(bound_ref.shape, f32) + bound


def face_end_kernel(sum_ref, start_ref, bound_ref, inv_ref):
    inv_ref[...] = start_ref[...]
    invert_end(sum_ref[...], jnp.max(bound_ref[...]), inv_ref)


def term_kernel(fold_ref, more_a, more_b, three_ref, data_ref, term_ref, known_ref):
    side, ncol = known_ref.shape
    rows = more_a.shape[0] - side
    for k in range(side // rows):
        lanes = slice(k * ncol, (k + 1) * ncol)
        known_ref[k * rows : (k + 1) * rows] = more_a[side:, lanes] + more_b[side:, lanes]
    term_ref[...] = mul(three_ref[...], data_ref[...]) - mul(fold_ref[:side], known_ref[...])


def rows_kernel(
    raw_any, one_ref, fold_ref, inv_ref, more_a, more_b, three_ref, rows_a, rows_b, base_a, base_b,
    outer, sem,
):
    side = inv_ref.shape[0]
    copy = pltpu.make_async_copy(
        raw_any.at[pl.ds(0, 2 * side), pl.ds(0, 2 * side)], outer, sem
    )
    copy.start()
    fold = parts_of(fold_ref[...])
    inner_a, inner_b = parts_of(more_a[:side]), parts_of(more_b[:side])
    rows_a[...] = -mul_parts(fold, inner_a)
    rows_a[:side] += three_ref[...]
    rows_b[...] = -mul_parts(fold, inner_b)
    left = parts_of(mul_parts(inner_a, parts_of(inv_ref[...]), ((0,), (0,))))
    base_b[...] = -mul_parts(left, inner_b)
    shape = (2 * side, 2 * side)
    copy.wait()
    level = jnp.where(rows_of(shape) == cols_of(shape), one_ref[side + 1 : side + 2, :], 0.0)
    base_a[...] = (outer[...] + level) - mul_parts(left, inner_a)


def near_kernel(
    inv2_ref, rows_a, rows_b, base_a, base_b, three_b, fold_ref, out_a, out_b, scaled_ref, mixed_ref
):
    side = three_b.shape[0]
    right = parts_of(rows_a[...])
    scaled = mul_parts(right, parts_of(inv2_ref[...]), ((0,), (0,)))
    scaled_ref[...] = scaled
    scaled = parts_of(scaled)
    mixed_ref[...] = mul_parts(scaled, parts_of(fold_ref[...]))
    out_a[...] = base_a[...] - mul_parts(scaled, right)
    sib = rows_b[...]
    sib = jnp.concatenate([sib[:side], sib[side:] + three_b[...]], axis=0)
    out_b[...] = base_b[...] - mul_parts(scaled, parts_of(sib))


def cross_kernel(scaled_ref, mixed_ref, two_c, two_d, three_c, out_c, out_d):
    side = two_c.shape[0]
    scaled = parts_of(scaled_ref[:, :side])
    mixed = parts_of(mixed_ref[...])
    out_c[...] = mul_parts(mixed, parts_of(two_c[...])) - mul_parts(scaled, parts_of(three_c[...]))
    out_d[...] = mul_parts(mixed, parts_of(two_d[...]))


def last_kernel(place_ref, out_a, out_b, out_c, part_d, scaled_ref, three_d, out_any, out_d, sems):
    side, width = three_d.shape
    copies = []
    for k, ref in enumerate((out_a, out_b, out_c, out_d)):
        lanes = pl.ds(pl.multiple_of(place_ref[k] * width, width), width)
        copies.append(pltpu.make_async_copy(ref, out_any.at[:, lanes], sems.at[k]))
    for copy in copies[:3]:
        copy.start()
    left = parts_of(scaled_ref[:, side:])
    out_d[...] = part_d[...] - mul_parts(left, parts_of(three_d[...]))
    copies[3].start()
    for copy in copies:
        copy.wait()


def values_kernel(total_own, total_sib, known_ref, inv_ref, inv2_ref, own_ref, sib_ref, out_ref):
    side = inv_ref.shape[0]
    face = -mul(inv2_ref[...], jnp.concatenate([total_own[...], total_sib[...]], axis=0))
    out_ref[:side] = face[:side]
    inner = (
        known_ref[...]
        + mul(own_ref[:side, side:], face[:side])
        + mul(sib_ref[:side, side:], face[side:])
    )
    out_ref[side:] = -mul(inv_ref[...], inner)


def call(kernel, outs, args, us, name, specs=None, out_specs=None, scratch=()):
    return pl.pallas_call(
        kernel,
        out_shape=[jax.ShapeDtypeStruct(s, f32) for s in outs],
        in_specs=specs or [VM] * len(args),
        out_specs=out_specs or [VM] * len(outs),
        scratch_shapes=[pltpu.VMEM(s, f32) if isinstance(s, tuple) else s for s in scratch],
        compiler_params=pltpu.CompilerParams(vmem_limit_bytes=12 * 1024 * 1024),
        cost_estimate=pl.CostEstimate(flops=int(us * 3e8), bytes_accessed=0, transcendentals=0),
        name=name,
    )(*args)


def in_hbm(array):
    return pltpu.with_memory_space_constraint(array, pltpu.HBM)


def after(arrays, done):
    return lax.optimization_barrier((*arrays, done))


def body(leaf_raw, medium_class, wave_table, boundary_data):
    raw = leaf_raw[0, 0]
    classes = medium_class[0, 0]
    data = boundary_data[0, 0]
    bound = raw.shape[0]
    side = bound // 4
    ncol = data.shape[1]
    half_x = lax.axis_size("gx") // 2
    half_y = lax.axis_size("gy") // 2
    column = lax.axis_index("gx") // half_x
    row = lax.axis_index("gy") // half_y
    place = jnp.stack(
        [2 * row + column, 2 * row + 1 - column, 2 - 2 * row + column, 3 - 2 * row - column]
    ).astype(jnp.int32)
    sq, sq2, wide, thin = (side, side), (2 * side, 2 * side), (side, 2 * side), (2 * side, side)
    narrow = (side, ncol)

    one, two, three, more = call(
        pack_kernel,
        [(side + 8, 2 * side), wide, wide, (side + ncol // 2, 2 * side)],
        tuple(in_hbm(x) for x in (classes, wave_table, raw, data)),
        2,
        "pack",
        specs=[HBM] * 4,
        scratch=[
            pltpu.SMEM(classes.shape, jnp.int32),
            pltpu.SMEM(wave_table.shape, f32),
            (2 * side, bound),
            data.shape,
            pltpu.SemaphoreType.DMA((4,)),
        ],
    )
    one_z = shifted(one, "gy")
    one_x = shifted(one, "gx")
    more_s, one_x = after((more,), one_x)
    more_x = shifted(more_s, "gx")
    inv1, fold1, face1 = call(
        own_kernel, [sq, thin, sq2], (one, one_x), 5, "own_level", scratch=[sq]
    )
    two_s, one_z, inv1 = after((two, one_z), inv1)
    two_z = shifted(two_s, "gy")
    one_zx = shifted(one_z, "gx")
    term, known = call(
        term_kernel, [narrow] * 2, (fold1, more, more_x, three, data), 1, "own_term"
    )
    three_s, more_x, term = after((three, more_x), term)
    three_z = shifted(three_s, "gy")
    rows_a, rows_b, base_a, base_b = call(
        rows_kernel,
        [sq2] * 4,
        (in_hbm(raw), one, fold1, inv1, more, more_x, three),
        2,
        "pair_rows",
        specs=[HBM] + [VM] * 6,
        scratch=[sq2, pltpu.SemaphoreType.DMA(())],
    )
    one_zx, rows_a = after((one_zx,), rows_a)
    three_s, one_zx = after((three,), one_zx)
    three_x = shifted(three_s, "gx")
    fold2, sum2 = call(
        far_kernel, [thin, sq2], (one_z, one_zx, face1), 6, "far_level", scratch=[sq, sq]
    )
    start2, bound2 = call(
        face_start_kernel, [sq2, (8, 128)], (one, sum2), 6, "face_start", scratch=[sq2]
    )
    term_s, start2 = after((term,), start2)
    term_z = shifted(term_s, "gy")
    two_z, start2 = after((two_z,), start2)
    two_zx = shifted(two_z, "gx")
    start2, two_z = after((start2,), two_z)
    (inv2,) = call(face_end_kernel, [sq2], (sum2, start2, bound2), 4, "face_end")
    three_z, inv2 = after((three_z,), inv2)
    three_zx = shifted(three_z, "gx")
    out_a, out_b, scaled, mixed = call(
        near_kernel,
        [sq2, sq2, sq2, thin],
        (inv2, rows_a, rows_b, base_a, base_b, three_x, fold2),
        3,
        "near_rows",
    )
    term_z, scaled = after((term_z,), scaled)
    total = term + term_z
    total_x = shifted(total, "gx")
    out_c, part_d = call(
        cross_kernel, [sq2, sq2], (scaled, mixed, two_z, two_zx, three_z), 2, "cross_rows"
    )
    (values,) = call(
        values_kernel,
        [(2 * side, ncol)],
        (total, total_x, known, inv1, inv2, one, one_x),
        2,
        "values",
    )
    (parent,) = call(
        last_kernel,
        [(2 * side, 8 * side)],
        (place, out_a, out_b, out_c, part_d, scaled, three_zx),
        2,
        "last_rows",
        specs=[SM] + [VM] * 6,
        out_specs=[ANY],
        scratch=[sq2, pltpu.SemaphoreType.DMA((4,))],
    )
    return (parent[None, None], values[None, None])


def solution(mesh):
    return jax.shard_map(
        body,
        mesh=mesh,
        in_specs=(P("gx", "gy", None, None), P("gx", "gy", None), P(), P("gx", "gy", None, None)),
        out_specs=(P("gx", "gy", None, None), P("gx", "gy", None, None)),
        check_vma=False,
    )
```

```python
import functools

import jax
import jax.numpy as jnp
from jax import lax
from jax.experimental import pallas as pl
from jax.experimental.pallas import tpu as pltpu
from jax.sharding import PartitionSpec as P

f32 = jnp.float32
bf16 = jnp.bfloat16
VM = pl.BlockSpec(memory_space=pltpu.VMEM)
ANY = pl.BlockSpec(memory_space=pl.ANY)
HBM = pl.BlockSpec(memory_space=pltpu.HBM)
SM = pl.BlockSpec(memory_space=pltpu.SMEM)
LEAST = 4.0


def shifted(shard, axis):
    size = lax.axis_size(axis)
    return lax.ppermute(shard, axis, [(i, (i + size // 2) % size) for i in range(size)])


def parts_of(x, count=2):
    parts = []
    for _ in range(count - 1):
        parts.append(x.astype(bf16))
        x = x - parts[-1].astype(f32)
    return parts + [x.astype(bf16)]


def dot_of(left, right, contract):
    return lax.dot_general(left, right, (contract, ((), ())), preferred_element_type=f32)


def mul_parts(left, right, contract=((1,), (0,))):
    depth = max(len(left), len(right))
    total = None
    for order in reversed(range(depth)):
        for i in range(order + 1):
            if i < len(left) and order - i < len(right):
                term = dot_of(left[i], right[order - i], contract)
                total = term if total is None else total + term
    return total


def mul(left, right):
    return mul_parts(parts_of(left), parts_of(right))


def mul_t(left, right):
    return mul_parts(parts_of(left), parts_of(right), ((0,), (0,)))


def rows_of(shape):
    return lax.broadcasted_iota(jnp.int32, shape, 0)


def cols_of(shape):
    return lax.broadcasted_iota(jnp.int32, shape, 1)


def eye(n):
    return (rows_of((n, n)) == cols_of((n, n))).astype(f32)


def invert_start(mat, least, inv_ref, res_ref):
    n = mat.shape[0]
    unit = eye(n)
    most = jnp.max(jnp.sum(jnp.abs(mat), axis=0, keepdims=True))
    scale = 2.0 / (most + least)
    eps = (most - least) / (most + least)
    res = unit - scale * mat
    gain = 2.0 / (2.0 - eps * eps)
    inv_ref[...] = (gain * scale) * (unit + res)
    res_parts = parts_of(res)
    res_ref[...] = (1.0 - gain) * unit + gain * mul_parts(res_parts, res_parts)

    def fast(carry):
        eps, noise = carry
        gain = 2.0 / (2.0 - eps * eps)
        inv = inv_ref[...]
        high, low = parts_of(res_ref[...])
        inv_high, inv_low = parts_of(inv)
        if n > 256:
            right_high = jnp.concatenate([high, inv_high], axis=1)
            right_low = jnp.concatenate([low, inv_low], axis=1)
            both = dot_of(
                jnp.concatenate([high, high, low], axis=1),
                jnp.concatenate([right_high, right_low, right_high], axis=0),
                ((1,), (0,)),
            )
            square, step = both[:, :n], both[:, n:]
        else:
            square = mul_parts([high, low], [high, low])
            step = mul_parts([high, low], [inv_high, inv_low])
        inv_ref[...] = gain * (inv + step)
        res_ref[...] = (1.0 - gain) * unit + gain * square
        return gain * eps * eps * 0.5, 2.0 * gain * eps * noise + 3e-5

    eps, noise = lax.while_loop(
        lambda carry: carry[0] > 0.02, fast, (gain * eps * eps * 0.5, jnp.float32(6e-5))
    )
    return jnp.minimum(eps + noise + 1e-5 * (most / least), 0.5)


def invert_end(mat, bound, inv_ref):
    unit = eye(mat.shape[0])
    mat_parts = parts_of(mat, 3)

    def residual(inv_parts):
        return unit - mul_parts(mat_parts, inv_parts)

    def correct(bound):
        inv = inv_ref[...]
        inv_parts = parts_of(inv, 3)
        inv_ref[...] = inv + mul_parts(inv_parts[:2], parts_of(residual(inv_parts)))
        return bound * bound

    lax.while_loop(lambda bound: bound > 0.01, correct, bound)
    inv = inv_ref[...]
    inv_parts = parts_of(inv, 3)
    res_parts = parts_of(residual(inv_parts))
    step = mul_parts(inv_parts[:2], res_parts)
    inv_ref[...] = inv + (step + dot_of(step.astype(bf16), res_parts[0], ((1,), (0,))))


def invert(mat, least, inv_ref, res_ref):
    invert_end(mat, invert_start(mat, least, inv_ref, res_ref), inv_ref)


def pack_kernel(
    class_any, table_any, raw_any, data_any, one_ref, two_ref, three_ref, four_ref, face_ref, more_ref,
    classes, table, raw, data, sems,
):
    bound = raw_any.shape[0]
    side = bound // 4
    blk = bound // class_any.shape[0]
    shape = (side, side)
    copies = [
        pltpu.make_async_copy(class_any, classes, sems.at[0]),
        pltpu.make_async_copy(table_any, table, sems.at[1]),
        pltpu.make_async_copy(raw_any.at[pl.ds(2 * side, 2 * side)], raw, sems.at[2]),
        pltpu.make_async_copy(data_any, data, sems.at[3]),
    ]
    for copy in copies:
        copy.start()
    row, col = rows_of(shape), cols_of(shape)
    for copy in copies:
        copy.wait()
    least = table[0]
    for k in range(1, table.shape[0]):
        least = jnp.minimum(least, table[k])

    def level_of(index, start, count):
        level = jnp.zeros(index.shape, f32)
        for k in range(count):
            level = jnp.where(index // blk == k, LEAST + table[classes[start + k]], level)
        return level

    def with_diagonal(block, start):
        return block + jnp.where(row == col, level_of(row, start // blk, side // blk), 0.0)

    face = with_diagonal(raw[:side, 2 * side : 3 * side], 2 * side)
    inner = with_diagonal(raw[side:, 3 * side :], 3 * side)
    one_ref[:side, :side] = jnp.where(row <= col, inner, face)
    one_ref[:side, side:] = raw[side:, 2 * side : 3 * side]
    one_ref[side : side + 8, :] = jnp.zeros((8, 2 * side), f32)
    one_ref[side : side + 1, :side] = jnp.sum(
        jnp.where(row == col, face, 0.0), axis=0, keepdims=True
    )
    one_ref[side + 1 : side + 2, :] = level_of(cols_of((1, 2 * side)), 0, 2 * side // blk)
    one_ref[side + 2 : side + 3, :] = jnp.zeros((1, 2 * side), f32) + 2.0 * (LEAST + least)
    inner_out = raw[side:, : 2 * side]
    face_ref[...] = raw[:side, : 2 * side]
    outer = jnp.concatenate([inner_out, raw[:side, : 2 * side]], axis=0)
    cut = 0
    for ref in (two_ref, three_ref, four_ref):
        ref[...] = outer[cut : cut + ref.shape[0]]
        cut = cut + ref.shape[0]
    more_ref[:side] = inner_out
    known = mul(inner_out, data[...])
    rows, ncol = more_ref.shape[0] - side, data.shape[1]
    for k in range(side // rows):
        more_ref[side:, k * ncol : (k + 1) * ncol] = known[k * rows : (k + 1) * rows]


def unpack(one_ref):
    side = one_ref.shape[1] // 2
    shape = (side, side)
    row, col = rows_of(shape), cols_of(shape)
    packed = one_ref[:side, :side]
    flipped = packed.T
    inner = jnp.where(row <= col, packed, flipped)
    face = jnp.where(row > col, packed, jnp.where(row < col, flipped, one_ref[side : side + 1, :side]))
    return inner, face, one_ref[:side, side:]


def least_of(one_ref):
    side = one_ref.shape[1] // 2
    return jnp.min(one_ref[side + 2 : side + 3, :])


def pair_level(own_ref, sib_ref, res, inv_ref, fold_ref):
    side = own_ref.shape[1] // 2
    inner_a, face_a, cross_a = unpack(own_ref)
    inner_b, face_b, cross_b = unpack(sib_ref)
    invert(inner_a + inner_b, least_of(own_ref), inv_ref, res)
    inv_parts = parts_of(inv_ref[...])
    parts_a, parts_b = parts_of(cross_a), parts_of(cross_b)
    fold_a = mul_parts(parts_a, inv_parts, ((0,), (0,)))
    fold_b = mul_parts(parts_b, inv_parts, ((0,), (0,)))
    fold_ref[:side] = fold_a
    fold_ref[side:] = fold_b
    fold_a, fold_b = parts_of(fold_a), parts_of(fold_b)
    aa = face_a - mul_parts(fold_a, parts_a)
    ab = -mul_parts(fold_a, parts_b)
    ba = -mul_parts(fold_b, parts_a)
    bb = face_b - mul_parts(fold_b, parts_b)
    return aa, ab, ba, bb


def own_kernel(own_ref, sib_ref, inv_ref, fold_ref, face_ref, res):
    side = own_ref.shape[1] // 2
    aa, ab, ba, bb = pair_level(own_ref, sib_ref, res, inv_ref, fold_ref)
    face_ref[:side, :side] = aa
    face_ref[:side, side:] = ab
    face_ref[side:, :side] = ba
    face_ref[side:, side:] = bb


def far_kernel(own_ref, sib_ref, near_ref, fold_ref, sum_ref, res, inv):
    side = own_ref.shape[1] // 2
    aa, ab, ba, bb = pair_level(own_ref, sib_ref, res, inv, fold_ref)
    sum_ref[:side, :side] = near_ref[:side, :side] + aa
    sum_ref[:side, side:] = near_ref[:side, side:] + ab
    sum_ref[side:, :side] = near_ref[side:, :side] + ba
    sum_ref[side:, side:] = near_ref[side:, side:] + bb


def face_start_kernel(own_ref, sum_ref, inv_ref, bound_ref, res):
    bound = invert_start(sum_ref[...], least_of(own_ref), inv_ref, res)
    bound_ref[...] = jnp.zeros(bound_ref.shape, f32) + bound


def face_end_kernel(sum_ref, start_ref, bound_ref, inv_ref):
    inv_ref[...] = start_ref[...]
    invert_end(sum_ref[...], jnp.max(bound_ref[...]), inv_ref)


def term_kernel(fold_ref, more_a, more_b, three_ref, data_ref, term_ref, known_ref):
    side, ncol = known_ref.shape
    rows = more_a.shape[0] - side
    for k in range(side // rows):
        lanes = slice(k * ncol, (k + 1) * ncol)
        known_ref[k * rows : (k + 1) * rows] = more_a[side:, lanes] + more_b[side:, lanes]
    term_ref[...] = mul(three_ref[...], data_ref[...]) - mul(fold_ref[:side], known_ref[...])


def rows_kernel(
    raw_any, one_ref, fold_ref, inv_ref, more_a, more_b, three_ref, known_ref,
    rows_a, rows_b, base_a, base_b, fold_any, shift_any, outer, shift, sems,
):
    side = inv_ref.shape[0]
    copy = pltpu.make_async_copy(
        raw_any.at[pl.ds(0, 2 * side), pl.ds(0, 2 * side)], outer, sems.at[0]
    )
    copy.start()
    fold_store = pltpu.make_async_copy(fold_ref, fold_any, sems.at[1])
    fold_store.start()
    fold = parts_of(fold_ref[...])
    inverse = parts_of(inv_ref[...])
    shift[...] = -mul_parts(inverse, parts_of(known_ref[...]))
    shift_store = pltpu.make_async_copy(shift, shift_any, sems.at[2])
    shift_store.start()
    inner_a, inner_b = parts_of(more_a[:side]), parts_of(more_b[:side])
    rows_a[...] = -mul_parts(fold, inner_a)
    rows_a[:side] += three_ref[...]
    rows_b[...] = -mul_parts(fold, inner_b)
    left = parts_of(mul_parts(inner_a, inverse, ((0,), (0,))))
    base_b[...] = -mul_parts(left, inner_b)
    shape = (2 * side, 2 * side)
    copy.wait()
    level = jnp.where(rows_of(shape) == cols_of(shape), one_ref[side + 1 : side + 2, :], 0.0)
    base_a[...] = (outer[...] + level) - mul_parts(left, inner_a)
    fold_store.wait()
    shift_store.wait()


def pieces(source, target, sems, start, lanes=slice(None), count=4):
    rows = source.shape[0] // count
    return [
        pltpu.make_async_copy(
            source.at[pl.ds(k * rows, rows)], target.at[pl.ds(k * rows, rows), lanes], sems.at[start + k]
        )
        for k in range(count)
    ]


def lanes_of(place_ref, k, width):
    return pl.ds(pl.multiple_of(place_ref[k] * width, width), width)


def start_all(copies):
    for copy in copies:
        copy.start()


def wait_all(copies):
    for copy in copies:
        copy.wait()


def near_kernel(
    inv2_ref, rows_a, rows_b, base_a, base_b, face_b, fold_ref, out_a, out_b, left_c, left_d
):
    side = face_b.shape[0]
    right = parts_of(rows_a[...])
    scaled = mul_parts(right, parts_of(inv2_ref[...]), ((0,), (0,)))
    left_c[:, side:] = -scaled[:, :side]
    left_d[:, side:] = -scaled[:, side:]
    scaled = parts_of(scaled)
    mixed = mul_parts(scaled, parts_of(fold_ref[...]))
    left_c[:, :side] = mixed
    left_d[:, :side] = mixed
    out_a[...] = base_a[...] - mul_parts(scaled, right)
    sib = rows_b[...]
    sib = jnp.concatenate([sib[:side], sib[side:] + face_b[...]], axis=0)
    out_b[...] = base_b[...] - mul_parts(scaled, parts_of(sib))


def cross_kernel(
    place_ref, fold_any, shift_any, out_a, out_b, left_c, left_d, two_c, three_c, four_c, two_d, three_d,
    inv2_ref, total_ref, out_any, part_d, map_ref, base_ref, out_c, fold, shift, sems,
):
    width = two_c.shape[1]
    side = width // 2
    stores = [
        pltpu.make_async_copy(ref, out_any.at[:, lanes_of(place_ref, k, width)], sems.at[k])
        for k, ref in enumerate((out_a, out_b, out_c))
    ]
    loads = [
        pltpu.make_async_copy(fold_any, fold, sems.at[3]),
        pltpu.make_async_copy(shift_any, shift, sems.at[4]),
    ]
    start_all(loads)
    start_all(stores[:2])
    out_c[...] = mul(left_c[...], jnp.concatenate([two_c[...], three_c[...], four_c[...]], axis=0))
    stores[2].start()
    far_d = jnp.concatenate([two_d[...], three_d[...]], axis=0)
    part_d[...] = mul(left_d[:, : far_d.shape[0]], far_d)
    wait_all(loads)
    upper = -inv2_ref[:side]
    lower = mul_t(fold[...], inv2_ref[...])
    map_ref[:side] = upper[:, side:]
    map_ref[side:] = lower[:, side:]
    total = parts_of(total_ref[...])
    base_ref[:side] = mul_parts(parts_of(upper[:, :side]), total)
    base_ref[side:] = mul_parts(parts_of(lower[:, :side]), total) + shift[...]
    wait_all(stores)


def last_kernel(
    place_ref, in_any, part_d, left_d, four_d, map_ref, base_ref, total_ref,
    out_any, values_any, out_d, values, sems,
):
    tail, width = four_d.shape
    right = parts_of(four_d[...])
    values[...] = base_ref[...] + mul(map_ref[...], total_ref[...])
    values_store = pltpu.make_async_copy(values, values_any, sems.at[4])
    values_store.start()
    stores = pieces(out_d, out_any, sems, 0, lanes_of(place_ref, 3, width))
    rows = width // len(stores)
    for k, store in enumerate(stores):
        part = slice(k * rows, (k + 1) * rows)
        out_d[part] = part_d[part] + mul_parts(parts_of(left_d[part, width - tail :]), right)
        store.start()
    wait_all(stores + [values_store])


COSTS = {'*': 1000000000, 'own_level': 1500000000, 'own_term': 300000000, 'far_level': 1800000000, 'face_start': 1800000000, 'face_end': 1200000000}


def call(kernel, outs, args, us, name, specs=None, out_specs=None, scratch=(), aliases=None):
    return pl.pallas_call(
        kernel,
        out_shape=[
            pltpu.HBM(s, f32) if spec is HBM else jax.ShapeDtypeStruct(s, f32)
            for s, spec in zip(outs, out_specs or [VM] * len(outs))
        ],
        in_specs=specs or [VM] * len(args),
        out_specs=out_specs or [VM] * len(outs),
        scratch_shapes=[pltpu.VMEM(s, f32) if isinstance(s, tuple) else s for s in scratch],
        compiler_params=pltpu.CompilerParams(vmem_limit_bytes=12 * 1024 * 1024),
        cost_estimate=pl.CostEstimate(flops=COSTS.get(name, COSTS["*"]), bytes_accessed=0, transcendentals=0),
        input_output_aliases=aliases or {},
        name=name,
    )(*args)


def in_hbm(array):
    return pltpu.with_memory_space_constraint(array, pltpu.HBM)


def after(arrays, done):
    return lax.optimization_barrier((*arrays, done))


def body(leaf_raw, medium_class, wave_table, boundary_data):
    raw = leaf_raw[0, 0]
    classes = medium_class[0, 0]
    data = boundary_data[0, 0]
    bound = raw.shape[0]
    side = bound // 4
    ncol = data.shape[1]
    half_x = lax.axis_size("gx") // 2
    half_y = lax.axis_size("gy") // 2
    column = lax.axis_index("gx") // half_x
    row = lax.axis_index("gy") // half_y
    place = jnp.stack(
        [2 * row + column, 2 * row + 1 - column, 2 - 2 * row + column, 3 - 2 * row - column]
    ).astype(jnp.int32)
    sq, sq2, wide, thin = (side, side), (2 * side, 2 * side), (side, 2 * side), (2 * side, side)
    narrow = (side, ncol)

    third = 2 * side // 3
    full = (2 * side, 8 * side)
    one, two, three, four, face, more = call(
        pack_kernel,
        [(side + 8, 2 * side)] + [(third, 2 * side)] * 3 + [wide, (side + ncol // 2, 2 * side)],
        tuple(in_hbm(x) for x in (classes, wave_table, raw, data)),
        2,
        "pack",
        specs=[HBM] * 4,
        scratch=[
            pltpu.SMEM(classes.shape, jnp.int32),
            pltpu.SMEM(wave_table.shape, f32),
            (2 * side, bound),
            data.shape,
            pltpu.SemaphoreType.DMA((4,)),
        ],
    )
    one_z = shifted(one, "gy")
    one_x = shifted(one, "gx")
    more_s, one_x = after((more,), one_x)
    more_x = shifted(more_s, "gx")
    inv1, fold1, face1 = call(
        own_kernel, [sq, thin, sq2], (one, one_x), 5, "own_level", scratch=[sq]
    )
    two_s, one_z, inv1 = after((two, one_z), inv1)
    two_z = shifted(two_s, "gy")
    one_zx = shifted(one_z, "gx")
    term, known = call(
        term_kernel, [narrow] * 2, (fold1, more, more_x, face, data), 1, "own_term"
    )
    three_s, more_x, term = after((three, more_x), term)
    three_z = shifted(three_s, "gy")
    rows_a, rows_b, base_a, base_b, fold_h, shift = call(
        rows_kernel,
        [sq2] * 4 + [thin, narrow],
        (in_hbm(raw), one, fold1, inv1, more, more_x, face, known),
        2,
        "pair_rows",
        specs=[HBM] + [VM] * 7,
        out_specs=[VM] * 4 + [HBM] * 2,
        scratch=[sq2, narrow, pltpu.SemaphoreType.DMA((3,))],
    )
    one_zx, rows_a = after((one_zx,), rows_a)
    face_s, one_zx = after((face,), one_zx)
    face_x = shifted(face_s, "gx")
    fold2, sum2 = call(
        far_kernel, [thin, sq2], (one_z, one_zx, face1), 6, "far_level", scratch=[sq, sq]
    )
    start2, bound2 = call(
        face_start_kernel, [sq2, (8, 128)], (one, sum2), 6, "face_start", scratch=[sq2]
    )
    two_z, start2 = after((two_z,), start2)
    two_zx = shifted(two_z, "gx")
    start2, two_z = after((start2,), two_z)
    four_s, term_s, start2 = after((four, term), start2)
    four_z = shifted(four_s, "gy")
    term_z = shifted(term_s, "gy")
    three_z, start2 = after((three_z,), start2)
    three_zx = shifted(three_z, "gx")
    start2, three_z = after((start2,), three_z)
    (inv2,) = call(face_end_kernel, [sq2], (sum2, start2, bound2), 4, "face_end")
    out_a, out_b, left_c, left_d = call(
        near_kernel,
        [sq2] * 4,
        (inv2, rows_a, rows_b, base_a, base_b, face_x, fold2),
        3,
        "near_rows",
    )
    four_z, left_c = after((four_z,), left_c)
    four_zx = shifted(four_z, "gx")
    term_z, four_z = after((term_z,), four_z)
    total = term + term_z
    total_x = shifted(total, "gx")
    parent, part_d, value_map, value_base = call(
        cross_kernel,
        [full, sq2, thin, (2 * side, ncol)],
        (
            place, in_hbm(fold_h), in_hbm(shift), out_a, out_b, left_c, left_d, two_z, three_z, four_z,
            two_zx, three_zx, inv2, total,
        ),
        2,
        "cross_rows",
        specs=[SM, HBM, HBM] + [VM] * 11,
        out_specs=[HBM, VM, VM, VM],
        scratch=[sq2, thin, narrow, pltpu.SemaphoreType.DMA((5,))],
    )
    parent, values = call(
        last_kernel,
        [full, (2 * side, ncol)],
        (place, in_hbm(parent), part_d, left_d, four_zx, value_map, value_base, total_x),
        2,
        "last_rows",
        specs=[SM, HBM] + [VM] * 6,
        out_specs=[HBM, HBM],
        scratch=[sq2, (2 * side, ncol), pltpu.SemaphoreType.DMA((5,))],
        aliases={1: 0},
    )
    return (parent[None, None], values[None, None])


def solution(mesh):
    return jax.shard_map(
        body,
        mesh=mesh,
        in_specs=(P("gx", "gy", None, None), P("gx", "gy", None), P(), P("gx", "gy", None, None)),
        out_specs=(P("gx", "gy", None, None), P("gx", "gy", None, None)),
        check_vma=False,
    )
```

```python
import functools

import jax
import jax.numpy as jnp
from jax import lax
from jax.experimental import pallas as pl
from jax.experimental.pallas import tpu as pltpu
from jax.sharding import PartitionSpec as P

f32 = jnp.float32
bf16 = jnp.bfloat16
VM = pl.BlockSpec(memory_space=pltpu.VMEM)
ANY = pl.BlockSpec(memory_space=pl.ANY)
HBM = pl.BlockSpec(memory_space=pltpu.HBM)
SM = pl.BlockSpec(memory_space=pltpu.SMEM)
LEAST = 4.0


def shifted(shard, axis):
    size = lax.axis_size(axis)
    return lax.ppermute(shard, axis, [(i, (i + size // 2) % size) for i in range(size)])


def parts_of(x, count=2):
    parts = []
    for _ in range(count - 1):
        parts.append(x.astype(bf16))
        x = x - parts[-1].astype(f32)
    return parts + [x.astype(bf16)]


def dot_of(left, right, contract):
    return lax.dot_general(left, right, (contract, ((), ())), preferred_element_type=f32)


def mul_parts(left, right, contract=((1,), (0,))):
    depth = max(len(left), len(right))
    total = None
    for order in reversed(range(depth)):
        for i in range(order + 1):
            if i < len(left) and order - i < len(right):
                term = dot_of(left[i], right[order - i], contract)
                total = term if total is None else total + term
    return total


def mul(left, right):
    return mul_parts(parts_of(left), parts_of(right))


def mul_t(left, right):
    return mul_parts(parts_of(left), parts_of(right), ((0,), (0,)))


def rows_of(shape):
    return lax.broadcasted_iota(jnp.int32, shape, 0)


def cols_of(shape):
    return lax.broadcasted_iota(jnp.int32, shape, 1)


def eye(n):
    return (rows_of((n, n)) == cols_of((n, n))).astype(f32)


def invert_start(mat, least, inv_ref, res_ref):
    n = mat.shape[0]
    unit = eye(n)
    most = jnp.max(jnp.sum(jnp.abs(mat), axis=0, keepdims=True))
    scale = 2.0 / (most + least)
    eps = (most - least) / (most + least)
    res = unit - scale * mat
    gain = 2.0 / (2.0 - eps * eps)
    inv_ref[...] = (gain * scale) * (unit + res)
    res_parts = parts_of(res)
    res_ref[...] = (1.0 - gain) * unit + gain * mul_parts(res_parts, res_parts)

    def fast(carry):
        eps, noise = carry
        gain = 2.0 / (2.0 - eps * eps)
        inv = inv_ref[...]
        high, low = parts_of(res_ref[...])
        inv_high, inv_low = parts_of(inv)
        if n > 256:
            right_high = jnp.concatenate([high, inv_high], axis=1)
            right_low = jnp.concatenate([low, inv_low], axis=1)
            both = dot_of(
                jnp.concatenate([high, high, low], axis=1),
                jnp.concatenate([right_high, right_low, right_high], axis=0),
                ((1,), (0,)),
            )
            square, step = both[:, :n], both[:, n:]
        else:
            square = mul_parts([high, low], [high, low])
            step = mul_parts([high, low], [inv_high, inv_low])
        inv_ref[...] = gain * (inv + step)
        res_ref[...] = (1.0 - gain) * unit + gain * square
        return gain * eps * eps * 0.5, 2.0 * gain * eps * noise + 3e-5

    eps, noise = lax.while_loop(
        lambda carry: carry[0] > 0.02, fast, (gain * eps * eps * 0.5, jnp.float32(6e-5))
    )
    return jnp.minimum(eps + noise + 1e-5 * (most / least), 0.5)


def invert_end(mat, bound, inv_ref):
    unit = eye(mat.shape[0])
    mat_parts = parts_of(mat, 3)

    def residual(inv_parts):
        return unit - mul_parts(mat_parts, inv_parts)

    def correct(bound):
        inv = inv_ref[...]
        inv_parts = parts_of(inv, 3)
        inv_ref[...] = inv + mul_parts(inv_parts[:2], parts_of(residual(inv_parts)))
        return bound * bound

    lax.while_loop(lambda bound: bound > 0.01, correct, bound)
    inv = inv_ref[...]
    inv_parts = parts_of(inv, 3)
    res_parts = parts_of(residual(inv_parts))
    step = mul_parts(inv_parts[:2], res_parts)
    inv_ref[...] = inv + (step + dot_of(step.astype(bf16), res_parts[0], ((1,), (0,))))


def invert(mat, least, inv_ref, res_ref):
    invert_end(mat, invert_start(mat, least, inv_ref, res_ref), inv_ref)


def pack_kernel(class_any, table_any, raw_any, one_ref, classes, table, raw, sems):
    bound = raw_any.shape[0]
    side = bound // 4
    blk = bound // class_any.shape[0]
    shape = (side, side)
    copies = [
        pltpu.make_async_copy(class_any, classes, sems.at[0]),
        pltpu.make_async_copy(table_any, table, sems.at[1]),
        pltpu.make_async_copy(
            raw_any.at[pl.ds(2 * side, 2 * side), pl.ds(2 * side, 2 * side)], raw, sems.at[2]
        ),
    ]
    start_all(copies)
    row, col = rows_of(shape), cols_of(shape)
    wait_all(copies)
    least = table[0]
    for k in range(1, table.shape[0]):
        least = jnp.minimum(least, table[k])

    def level_of(index, start, count):
        level = jnp.zeros(index.shape, f32)
        for k in range(count):
            level = jnp.where(index // blk == k, LEAST + table[classes[start + k]], level)
        return level

    def with_diagonal(block, start):
        return block + jnp.where(row == col, level_of(row, start // blk, side // blk), 0.0)

    face = with_diagonal(raw[:side, :side], 2 * side)
    inner = with_diagonal(raw[side:, side:], 3 * side)
    one_ref[:side, :side] = jnp.where(row <= col, inner, face)
    one_ref[:side, side:] = raw[side:, :side]
    one_ref[side : side + 8, :] = jnp.zeros((8, 2 * side), f32)
    one_ref[side : side + 1, :side] = jnp.sum(
        jnp.where(row == col, face, 0.0), axis=0, keepdims=True
    )
    one_ref[side + 1 : side + 2, :] = level_of(cols_of((1, 2 * side)), 0, 2 * side // blk)
    one_ref[side + 2 : side + 3, :] = jnp.zeros((1, 2 * side), f32) + 2.0 * (LEAST + least)


def outer_kernel(raw_any, data_any, two_ref, three_ref, four_ref, face_ref, more_ref, raw, data, sems):
    side = raw.shape[0] // 2
    copies = [
        pltpu.make_async_copy(raw_any.at[pl.ds(2 * side, 2 * side), pl.ds(0, 2 * side)], raw, sems.at[0]),
        pltpu.make_async_copy(data_any, data, sems.at[1]),
    ]
    start_all(copies)
    wait_all(copies)
    inner_out = raw[side:]
    face_ref[...] = raw[:side]
    outer = jnp.concatenate([inner_out, raw[:side]], axis=0)
    third = two_ref.shape[0]
    for k, ref in enumerate((two_ref, three_ref, four_ref)):
        ref[...] = outer[k * third : (k + 1) * third]
    more_ref[:side] = inner_out
    known = mul(inner_out, data[...])
    rows, ncol = more_ref.shape[0] - side, data.shape[1]
    for k in range(side // rows):
        more_ref[side:, k * ncol : (k + 1) * ncol] = known[k * rows : (k + 1) * rows]


def unpack(one_ref):
    side = one_ref.shape[1] // 2
    shape = (side, side)
    row, col = rows_of(shape), cols_of(shape)
    packed = one_ref[:side, :side]
    flipped = packed.T
    inner = jnp.where(row <= col, packed, flipped)
    face = jnp.where(row > col, packed, jnp.where(row < col, flipped, one_ref[side : side + 1, :side]))
    return inner, face, one_ref[:side, side:]


def least_of(one_ref):
    side = one_ref.shape[1] // 2
    return jnp.min(one_ref[side + 2 : side + 3, :])


def pair_level(own_ref, sib_ref, res, inv_ref, fold_ref):
    side = own_ref.shape[1] // 2
    inner_a, face_a, cross_a = unpack(own_ref)
    inner_b, face_b, cross_b = unpack(sib_ref)
    invert(inner_a + inner_b, least_of(own_ref), inv_ref, res)
    inv_parts = parts_of(inv_ref[...])
    parts_a, parts_b = parts_of(cross_a), parts_of(cross_b)
    fold_a = mul_parts(parts_a, inv_parts, ((0,), (0,)))
    fold_b = mul_parts(parts_b, inv_parts, ((0,), (0,)))
    fold_ref[:side] = fold_a
    fold_ref[side:] = fold_b
    fold_a, fold_b = parts_of(fold_a), parts_of(fold_b)
    aa = face_a - mul_parts(fold_a, parts_a)
    ab = -mul_parts(fold_a, parts_b)
    ba = -mul_parts(fold_b, parts_a)
    bb = face_b - mul_parts(fold_b, parts_b)
    return aa, ab, ba, bb


def own_kernel(own_ref, sib_ref, inv_ref, fold_ref, face_ref, res):
    side = own_ref.shape[1] // 2
    aa, ab, ba, bb = pair_level(own_ref, sib_ref, res, inv_ref, fold_ref)
    face_ref[:side, :side] = aa
    face_ref[:side, side:] = ab
    face_ref[side:, :side] = ba
    face_ref[side:, side:] = bb


def far_kernel(own_ref, sib_ref, near_ref, fold_ref, sum_ref, res, inv):
    side = own_ref.shape[1] // 2
    aa, ab, ba, bb = pair_level(own_ref, sib_ref, res, inv, fold_ref)
    sum_ref[:side, :side] = near_ref[:side, :side] + aa
    sum_ref[:side, side:] = near_ref[:side, side:] + ab
    sum_ref[side:, :side] = near_ref[side:, :side] + ba
    sum_ref[side:, side:] = near_ref[side:, side:] + bb


def face_start_kernel(own_ref, sum_ref, inv_ref, bound_ref, res):
    bound = invert_start(sum_ref[...], least_of(own_ref), inv_ref, res)
    bound_ref[...] = jnp.zeros(bound_ref.shape, f32) + bound


def face_end_kernel(sum_ref, start_ref, bound_ref, inv_ref):
    inv_ref[...] = start_ref[...]
    invert_end(sum_ref[...], jnp.max(bound_ref[...]), inv_ref)


def term_kernel(fold_ref, more_a, more_b, three_ref, data_ref, term_ref, known_ref):
    side, ncol = known_ref.shape
    rows = more_a.shape[0] - side
    for k in range(side // rows):
        lanes = slice(k * ncol, (k + 1) * ncol)
        known_ref[k * rows : (k + 1) * rows] = more_a[side:, lanes] + more_b[side:, lanes]
    term_ref[...] = mul(three_ref[...], data_ref[...]) - mul(fold_ref[:side], known_ref[...])


def rows_kernel(
    raw_any, one_ref, fold_ref, inv_ref, more_a, more_b, three_ref, known_ref,
    rows_a, rows_b, base_a, base_b, fold_any, shift_any, outer, shift, sems,
):
    side = inv_ref.shape[0]
    copy = pltpu.make_async_copy(
        raw_any.at[pl.ds(0, 2 * side), pl.ds(0, 2 * side)], outer, sems.at[0]
    )
    copy.start()
    fold_store = pltpu.make_async_copy(fold_ref, fold_any, sems.at[1])
    fold_store.start()
    fold = parts_of(fold_ref[...])
    inverse = parts_of(inv_ref[...])
    shift[...] = -mul_parts(inverse, parts_of(known_ref[...]))
    shift_store = pltpu.make_async_copy(shift, shift_any, sems.at[2])
    shift_store.start()
    inner_a, inner_b = parts_of(more_a[:side]), parts_of(more_b[:side])
    rows_a[...] = -mul_parts(fold, inner_a)
    rows_a[:side] += three_ref[...]
    rows_b[...] = -mul_parts(fold, inner_b)
    left = parts_of(mul_parts(inner_a, inverse, ((0,), (0,))))
    base_b[...] = -mul_parts(left, inner_b)
    shape = (2 * side, 2 * side)
    copy.wait()
    level = jnp.where(rows_of(shape) == cols_of(shape), one_ref[side + 1 : side + 2, :], 0.0)
    base_a[...] = (outer[...] + level) - mul_parts(left, inner_a)
    fold_store.wait()
    shift_store.wait()


def pieces(source, target, sems, start, lanes=slice(None), count=4):
    rows = source.shape[0] // count
    return [
        pltpu.make_async_copy(
            source.at[pl.ds(k * rows, rows)], target.at[pl.ds(k * rows, rows), lanes], sems.at[start + k]
        )
        for k in range(count)
    ]


def lanes_of(place_ref, k, width):
    return pl.ds(pl.multiple_of(place_ref[k] * width, width), width)


def start_all(copies):
    for copy in copies:
        copy.start()


def wait_all(copies):
    for copy in copies:
        copy.wait()


def near_kernel(
    inv2_ref, rows_a, rows_b, base_a, base_b, face_b, fold_ref, out_a, out_b, left_c, left_d
):
    side = face_b.shape[0]
    right = parts_of(rows_a[...])
    scaled = mul_parts(right, parts_of(inv2_ref[...]), ((0,), (0,)))
    left_c[:, side:] = -scaled[:, :side]
    left_d[:, side:] = -scaled[:, side:]
    scaled = parts_of(scaled)
    mixed = mul_parts(scaled, parts_of(fold_ref[...]))
    left_c[:, :side] = mixed
    left_d[:, :side] = mixed
    out_a[...] = base_a[...] - mul_parts(scaled, right)
    sib = rows_b[...]
    sib = jnp.concatenate([sib[:side], sib[side:] + face_b[...]], axis=0)
    out_b[...] = base_b[...] - mul_parts(scaled, parts_of(sib))


def cross_kernel(
    place_ref, fold_any, shift_any, out_a, out_b, left_c, left_d, two_c, three_c, four_c, two_d, three_d,
    inv2_ref, total_ref, out_any, part_d, map_ref, base_ref, out_c, fold, shift, sems,
):
    width = two_c.shape[1]
    side = width // 2
    stores = [
        pltpu.make_async_copy(ref, out_any.at[:, lanes_of(place_ref, k, width)], sems.at[k])
        for k, ref in enumerate((out_a, out_b, out_c))
    ]
    loads = [
        pltpu.make_async_copy(fold_any, fold, sems.at[3]),
        pltpu.make_async_copy(shift_any, shift, sems.at[4]),
    ]
    start_all(loads)
    start_all(stores[:2])
    out_c[...] = mul(left_c[...], jnp.concatenate([two_c[...], three_c[...], four_c[...]], axis=0))
    stores[2].start()
    far_d = jnp.concatenate([two_d[...], three_d[...]], axis=0)
    part_d[...] = mul(left_d[:, : far_d.shape[0]], far_d)
    wait_all(loads)
    upper = -inv2_ref[:side]
    lower = mul_t(fold[...], inv2_ref[...])
    map_ref[:side] = upper[:, side:]
    map_ref[side:] = lower[:, side:]
    total = parts_of(total_ref[...])
    base_ref[:side] = mul_parts(parts_of(upper[:, :side]), total)
    base_ref[side:] = mul_parts(parts_of(lower[:, :side]), total) + shift[...]
    wait_all(stores)


def last_kernel(
    place_ref, in_any, part_d, left_d, four_d, map_ref, base_ref, total_ref,
    out_any, values_any, out_d, values, sems,
):
    tail, width = four_d.shape
    right = parts_of(four_d[...])
    values[...] = base_ref[...] + mul(map_ref[...], total_ref[...])
    values_store = pltpu.make_async_copy(values, values_any, sems.at[4])
    values_store.start()
    stores = pieces(out_d, out_any, sems, 0, lanes_of(place_ref, 3, width))
    rows = width // len(stores)
    for k, store in enumerate(stores):
        part = slice(k * rows, (k + 1) * rows)
        out_d[part] = part_d[part] + mul_parts(parts_of(left_d[part, width - tail :]), right)
        store.start()
    wait_all(stores + [values_store])


COSTS = {'*': 1000000000, 'own_level': 1500000000, 'own_term': 300000000, 'far_level': 1800000000, 'face_start': 1800000000, 'face_end': 1200000000}


def call(kernel, outs, args, us, name, specs=None, out_specs=None, scratch=(), aliases=None):
    return pl.pallas_call(
        kernel,
        out_shape=[
            pltpu.HBM(s, f32) if spec is HBM else jax.ShapeDtypeStruct(s, f32)
            for s, spec in zip(outs, out_specs or [VM] * len(outs))
        ],
        in_specs=specs or [VM] * len(args),
        out_specs=out_specs or [VM] * len(outs),
        scratch_shapes=[pltpu.VMEM(s, f32) if isinstance(s, tuple) else s for s in scratch],
        compiler_params=pltpu.CompilerParams(vmem_limit_bytes=12 * 1024 * 1024),
        cost_estimate=pl.CostEstimate(flops=COSTS.get(name, COSTS["*"]), bytes_accessed=0, transcendentals=0),
        input_output_aliases=aliases or {},
        name=name,
    )(*args)


def in_hbm(array):
    return pltpu.with_memory_space_constraint(array, pltpu.HBM)


def after(arrays, done):
    return lax.optimization_barrier((*arrays, done))


def body(leaf_raw, medium_class, wave_table, boundary_data):
    raw = leaf_raw[0, 0]
    classes = medium_class[0, 0]
    data = boundary_data[0, 0]
    bound = raw.shape[0]
    side = bound // 4
    ncol = data.shape[1]
    half_x = lax.axis_size("gx") // 2
    half_y = lax.axis_size("gy") // 2
    column = lax.axis_index("gx") // half_x
    row = lax.axis_index("gy") // half_y
    place = jnp.stack(
        [2 * row + column, 2 * row + 1 - column, 2 - 2 * row + column, 3 - 2 * row - column]
    ).astype(jnp.int32)
    sq, sq2, wide, thin = (side, side), (2 * side, 2 * side), (side, 2 * side), (2 * side, side)
    narrow = (side, ncol)

    third = 2 * side // 3
    full = (2 * side, 8 * side)
    (one,) = call(
        pack_kernel,
        [(side + 8, 2 * side)],
        tuple(in_hbm(x) for x in (classes, wave_table, raw)),
        1,
        "pack",
        specs=[HBM] * 3,
        scratch=[
            pltpu.SMEM(classes.shape, jnp.int32),
            pltpu.SMEM(wave_table.shape, f32),
            sq2,
            pltpu.SemaphoreType.DMA((3,)),
        ],
    )
    two, three, four, face, more = call(
        outer_kernel,
        [(third, 2 * side)] * 3 + [wide, (side + ncol // 2, 2 * side)],
        tuple(in_hbm(x) for x in (raw, data)),
        1,
        "outer",
        specs=[HBM] * 2,
        scratch=[sq2, data.shape, pltpu.SemaphoreType.DMA((2,))],
    )
    one_z = shifted(one, "gy")
    one_x = shifted(one, "gx")
    more_s, one_x = after((more,), one_x)
    more_x = shifted(more_s, "gx")
    inv1, fold1, face1 = call(
        own_kernel, [sq, thin, sq2], (one, one_x), 5, "own_level", scratch=[sq]
    )
    two_s, one_z, inv1 = after((two, one_z), inv1)
    two_z = shifted(two_s, "gy")
    one_zx = shifted(one_z, "gx")
    term, known = call(
        term_kernel, [narrow] * 2, (fold1, more, more_x, face, data), 1, "own_term"
    )
    three_s, more_x, term = after((three, more_x), term)
    three_z = shifted(three_s, "gy")
    rows_a, rows_b, base_a, base_b, fold_h, shift = call(
        rows_kernel,
        [sq2] * 4 + [thin, narrow],
        (in_hbm(raw), one, fold1, inv1, more, more_x, face, known),
        2,
        "pair_rows",
        specs=[HBM] + [VM] * 7,
        out_specs=[VM] * 4 + [HBM] * 2,
        scratch=[sq2, narrow, pltpu.SemaphoreType.DMA((3,))],
    )
    one_zx, rows_a = after((one_zx,), rows_a)
    face_s, one_zx = after((face,), one_zx)
    face_x = shifted(face_s, "gx")
    fold2, sum2 = call(
        far_kernel, [thin, sq2], (one_z, one_zx, face1), 6, "far_level", scratch=[sq, sq]
    )
    start2, bound2 = call(
        face_start_kernel, [sq2, (8, 128)], (one, sum2), 6, "face_start", scratch=[sq2]
    )
    two_z, start2 = after((two_z,), start2)
    two_zx = shifted(two_z, "gx")
    start2, two_z = after((start2,), two_z)
    four_s, term_s, start2 = after((four, term), start2)
    four_z = shifted(four_s, "gy")
    term_z = shifted(term_s, "gy")
    three_z, start2 = after((three_z,), start2)
    three_zx = shifted(three_z, "gx")
    start2, three_z = after((start2,), three_z)
    (inv2,) = call(face_end_kernel, [sq2], (sum2, start2, bound2), 4, "face_end")
    out_a, out_b, left_c, left_d = call(
        near_kernel,
        [sq2] * 4,
        (inv2, rows_a, rows_b, base_a, base_b, face_x, fold2),
        3,
        "near_rows",
    )
    term_z, left_c = after((term_z,), left_c)
    total = term + term_z
    total_x = shifted(total, "gx")
    four_z, total = after((four_z,), total)
    four_zx = shifted(four_z, "gx")
    parent, part_d, value_map, value_base = call(
        cross_kernel,
        [full, sq2, thin, (2 * side, ncol)],
        (
            place, in_hbm(fold_h), in_hbm(shift), out_a, out_b, left_c, left_d, two_z, three_z, four_z,
            two_zx, three_zx, inv2, total,
        ),
        2,
        "cross_rows",
        specs=[SM, HBM, HBM] + [VM] * 11,
        out_specs=[HBM, VM, VM, VM],
        scratch=[sq2, thin, narrow, pltpu.SemaphoreType.DMA((5,))],
    )
    parent, values = call(
        last_kernel,
        [full, (2 * side, ncol)],
        (place, in_hbm(parent), part_d, left_d, four_zx, value_map, value_base, total_x),
        2,
        "last_rows",
        specs=[SM, HBM] + [VM] * 6,
        out_specs=[HBM, HBM],
        scratch=[sq2, (2 * side, ncol), pltpu.SemaphoreType.DMA((5,))],
        aliases={1: 0},
    )
    return (parent[None, None], values[None, None])


def solution(mesh):
    return jax.shard_map(
        body,
        mesh=mesh,
        in_specs=(P("gx", "gy", None, None), P("gx", "gy", None), P(), P("gx", "gy", None, None)),
        out_specs=(P("gx", "gy", None, None), P("gx", "gy", None, None)),
        check_vma=False,
    )
```

```python
import functools

import jax
import jax.numpy as jnp
from jax import lax
from jax.experimental import pallas as pl
from jax.experimental.pallas import tpu as pltpu
from jax.sharding import PartitionSpec as P

f32 = jnp.float32
bf16 = jnp.bfloat16
VM = pl.BlockSpec(memory_space=pltpu.VMEM)
ANY = pl.BlockSpec(memory_space=pl.ANY)
HBM = pl.BlockSpec(memory_space=pltpu.HBM)
SM = pl.BlockSpec(memory_space=pltpu.SMEM)
LEAST = 4.0


def shifted(shard, axis):
    size = lax.axis_size(axis)
    return lax.ppermute(shard, axis, [(i, (i + size // 2) % size) for i in range(size)])


def parts_of(x, count=2):
    parts = []
    for _ in range(count - 1):
        parts.append(x.astype(bf16))
        x = x - parts[-1].astype(f32)
    return parts + [x.astype(bf16)]


def dot_of(left, right, contract):
    return lax.dot_general(left, right, (contract, ((), ())), preferred_element_type=f32)


def mul_parts(left, right, contract=((1,), (0,))):
    depth = max(len(left), len(right))
    total = None
    for order in reversed(range(depth)):
        for i in range(order + 1):
            if i < len(left) and order - i < len(right):
                term = dot_of(left[i], right[order - i], contract)
                total = term if total is None else total + term
    return total


def mul(left, right):
    return mul_parts(parts_of(left), parts_of(right))


def mul_t(left, right):
    return mul_parts(parts_of(left), parts_of(right), ((0,), (0,)))


def rows_of(shape):
    return lax.broadcasted_iota(jnp.int32, shape, 0)


def cols_of(shape):
    return lax.broadcasted_iota(jnp.int32, shape, 1)


def eye(n):
    return (rows_of((n, n)) == cols_of((n, n))).astype(f32)


def invert_start(mat, least, inv_ref, res_ref, enough=0.02):
    n = mat.shape[0]
    unit = eye(n)
    most = jnp.max(jnp.sum(jnp.abs(mat), axis=0, keepdims=True))
    scale = 2.0 / (most + least)
    eps = (most - least) / (most + least)
    res = unit - scale * mat
    gain = 2.0 / (2.0 - eps * eps)
    inv_ref[...] = (gain * scale) * (unit + res)
    res_parts = parts_of(res)
    res_ref[...] = (1.0 - gain) * unit + gain * mul_parts(res_parts, res_parts)

    def fast(carry):
        eps, noise = carry
        gain = 2.0 / (2.0 - eps * eps)
        inv = inv_ref[...]
        high, low = parts_of(res_ref[...])
        inv_high, inv_low = parts_of(inv)
        if n > 256:
            right_high = jnp.concatenate([high, inv_high], axis=1)
            right_low = jnp.concatenate([low, inv_low], axis=1)
            both = dot_of(
                jnp.concatenate([high, high, low], axis=1),
                jnp.concatenate([right_high, right_low, right_high], axis=0),
                ((1,), (0,)),
            )
            square, step = both[:, :n], both[:, n:]
        else:
            square = mul_parts([high, low], [high, low])
            step = mul_parts([high, low], [inv_high, inv_low])
        inv_ref[...] = gain * (inv + step)
        res_ref[...] = (1.0 - gain) * unit + gain * square
        return gain * eps * eps * 0.5, 2.0 * gain * eps * noise + 3e-5

    eps, noise = lax.while_loop(
        lambda carry: carry[0] > enough, fast, (gain * eps * eps * 0.5, jnp.float32(6e-5))
    )
    return jnp.minimum(eps + noise + 1e-5 * (most / least), 0.5)


def invert_end(mat, bound, inv_ref):
    unit = eye(mat.shape[0])
    mat_parts = parts_of(mat, 3)

    def residual(inv_parts):
        return unit - mul_parts(mat_parts, inv_parts)

    def correct(bound):
        inv = inv_ref[...]
        inv_parts = parts_of(inv, 3)
        inv_ref[...] = inv + mul_parts(inv_parts[:2], parts_of(residual(inv_parts)))
        return bound * bound

    lax.while_loop(lambda bound: bound > 0.01, correct, bound)
    inv = inv_ref[...]
    inv_parts = parts_of(inv, 3)
    res_parts = parts_of(residual(inv_parts))
    step = mul_parts(inv_parts[:2], res_parts)
    inv_ref[...] = inv + (step + dot_of(step.astype(bf16), res_parts[0], ((1,), (0,))))


def invert(mat, least, inv_ref, res_ref):
    invert_end(mat, invert_start(mat, least, inv_ref, res_ref), inv_ref)


def pack_kernel(class_any, table_any, raw_any, one_ref, classes, table, raw, sems):
    bound = raw_any.shape[0]
    side = bound // 4
    blk = bound // class_any.shape[0]
    shape = (side, side)
    copies = [
        pltpu.make_async_copy(class_any, classes, sems.at[0]),
        pltpu.make_async_copy(table_any, table, sems.at[1]),
        pltpu.make_async_copy(
            raw_any.at[pl.ds(2 * side, 2 * side), pl.ds(2 * side, 2 * side)], raw, sems.at[2]
        ),
    ]
    start_all(copies)
    row, col = rows_of(shape), cols_of(shape)
    wait_all(copies)
    least = table[0]
    for k in range(1, table.shape[0]):
        least = jnp.minimum(least, table[k])

    def level_of(index, start, count):
        level = jnp.zeros(index.shape, f32)
        for k in range(count):
            level = jnp.where(index // blk == k, LEAST + table[classes[start + k]], level)
        return level

    def with_diagonal(block, start):
        return block + jnp.where(row == col, level_of(row, start // blk, side // blk), 0.0)

    face = with_diagonal(raw[:side, :side], 2 * side)
    inner = with_diagonal(raw[side:, side:], 3 * side)
    one_ref[:side, :side] = jnp.where(row <= col, inner, face)
    one_ref[:side, side:] = raw[side:, :side]
    one_ref[side : side + 8, :] = jnp.zeros((8, 2 * side), f32)
    one_ref[side : side + 1, :side] = jnp.sum(
        jnp.where(row == col, face, 0.0), axis=0, keepdims=True
    )
    one_ref[side + 1 : side + 2, :] = level_of(cols_of((1, 2 * side)), 0, 2 * side // blk)
    one_ref[side + 2 : side + 3, :] = jnp.zeros((1, 2 * side), f32) + 2.0 * (LEAST + least)


def outer_kernel(raw_any, data_any, two_ref, three_ref, four_ref, face_ref, more_ref, raw, data, sems):
    side = raw.shape[0] // 2
    copies = [
        pltpu.make_async_copy(raw_any.at[pl.ds(2 * side, 2 * side), pl.ds(0, 2 * side)], raw, sems.at[0]),
        pltpu.make_async_copy(data_any, data, sems.at[1]),
    ]
    start_all(copies)
    wait_all(copies)
    inner_out = raw[side:]
    face_ref[...] = raw[:side]
    outer = jnp.concatenate([inner_out, raw[:side]], axis=0)
    third = two_ref.shape[0]
    for k, ref in enumerate((two_ref, three_ref, four_ref)):
        ref[...] = outer[k * third : (k + 1) * third]
    more_ref[:side] = inner_out
    known = mul(inner_out, data[...])
    rows, ncol = more_ref.shape[0] - side, data.shape[1]
    for k in range(side // rows):
        more_ref[side:, k * ncol : (k + 1) * ncol] = known[k * rows : (k + 1) * rows]


def unpack(one_ref):
    side = one_ref.shape[1] // 2
    shape = (side, side)
    row, col = rows_of(shape), cols_of(shape)
    packed = one_ref[:side, :side]
    flipped = packed.T
    inner = jnp.where(row <= col, packed, flipped)
    face = jnp.where(row > col, packed, jnp.where(row < col, flipped, one_ref[side : side + 1, :side]))
    return inner, face, one_ref[:side, side:]


def least_of(one_ref):
    side = one_ref.shape[1] // 2
    return jnp.min(one_ref[side + 2 : side + 3, :])


def pair_level(own_ref, sib_ref, res, inv_ref, fold_ref):
    side = own_ref.shape[1] // 2
    inner_a, face_a, cross_a = unpack(own_ref)
    inner_b, face_b, cross_b = unpack(sib_ref)
    invert(inner_a + inner_b, least_of(own_ref), inv_ref, res)
    inv_parts = parts_of(inv_ref[...])
    parts_a, parts_b = parts_of(cross_a), parts_of(cross_b)
    fold_a = mul_parts(parts_a, inv_parts, ((0,), (0,)))
    fold_b = mul_parts(parts_b, inv_parts, ((0,), (0,)))
    fold_ref[:side] = fold_a
    fold_ref[side:] = fold_b
    fold_a, fold_b = parts_of(fold_a), parts_of(fold_b)
    aa = face_a - mul_parts(fold_a, parts_a)
    ab = -mul_parts(fold_a, parts_b)
    ba = -mul_parts(fold_b, parts_a)
    bb = face_b - mul_parts(fold_b, parts_b)
    return aa, ab, ba, bb


def own_kernel(own_ref, sib_ref, inv_ref, fold_ref, face_ref, res):
    side = own_ref.shape[1] // 2
    aa, ab, ba, bb = pair_level(own_ref, sib_ref, res, inv_ref, fold_ref)
    face_ref[:side, :side] = aa
    face_ref[:side, side:] = ab
    face_ref[side:, :side] = ba
    face_ref[side:, side:] = bb


def far_kernel(own_ref, sib_ref, near_ref, fold_ref, sum_ref, res, inv):
    side = own_ref.shape[1] // 2
    aa, ab, ba, bb = pair_level(own_ref, sib_ref, res, inv, fold_ref)
    sum_ref[:side, :side] = near_ref[:side, :side] + aa
    sum_ref[:side, side:] = near_ref[:side, side:] + ab
    sum_ref[side:, :side] = near_ref[side:, :side] + ba
    sum_ref[side:, side:] = near_ref[side:, side:] + bb


def face_start_kernel(own_ref, sum_ref, inv_ref, bound_ref, res):
    bound = invert_start(sum_ref[...], least_of(own_ref), inv_ref, res, 0.1)
    bound_ref[...] = jnp.zeros(bound_ref.shape, f32) + bound


def face_end_kernel(sum_ref, start_ref, bound_ref, inv_ref):
    inv_ref[...] = start_ref[...]
    invert_end(sum_ref[...], jnp.max(bound_ref[...]), inv_ref)


def term_kernel(fold_ref, more_a, more_b, three_ref, data_ref, term_ref, known_ref):
    side, ncol = known_ref.shape
    rows = more_a.shape[0] - side
    for k in range(side // rows):
        lanes = slice(k * ncol, (k + 1) * ncol)
        known_ref[k * rows : (k + 1) * rows] = more_a[side:, lanes] + more_b[side:, lanes]
    term_ref[...] = mul(three_ref[...], data_ref[...]) - mul(fold_ref[:side], known_ref[...])


def rows_kernel(
    raw_any, one_ref, fold_ref, inv_ref, more_a, more_b, three_ref, known_ref,
    rows_a, rows_b, base_a, base_b, fold_any, shift_any, outer, shift, sems,
):
    side = inv_ref.shape[0]
    copy = pltpu.make_async_copy(
        raw_any.at[pl.ds(0, 2 * side), pl.ds(0, 2 * side)], outer, sems.at[0]
    )
    copy.start()
    fold_store = pltpu.make_async_copy(fold_ref, fold_any, sems.at[1])
    fold_store.start()
    fold = parts_of(fold_ref[...])
    inverse = parts_of(inv_ref[...])
    shift[...] = -mul_parts(inverse, parts_of(known_ref[...]))
    shift_store = pltpu.make_async_copy(shift, shift_any, sems.at[2])
    shift_store.start()
    inner_a, inner_b = parts_of(more_a[:side]), parts_of(more_b[:side])
    rows_a[...] = -mul_parts(fold, inner_a)
    rows_a[:side] += three_ref[...]
    rows_b[...] = -mul_parts(fold, inner_b)
    left = parts_of(mul_parts(inner_a, inverse, ((0,), (0,))))
    base_b[...] = -mul_parts(left, inner_b)
    shape = (2 * side, 2 * side)
    copy.wait()
    level = jnp.where(rows_of(shape) == cols_of(shape), one_ref[side + 1 : side + 2, :], 0.0)
    base_a[...] = (outer[...] + level) - mul_parts(left, inner_a)
    fold_store.wait()
    shift_store.wait()


def pieces(source, target, sems, start, lanes=slice(None), count=4):
    rows = source.shape[0] // count
    return [
        pltpu.make_async_copy(
            source.at[pl.ds(k * rows, rows)], target.at[pl.ds(k * rows, rows), lanes], sems.at[start + k]
        )
        for k in range(count)
    ]


def lanes_of(place_ref, k, width):
    return pl.ds(pl.multiple_of(place_ref[k] * width, width), width)


def start_all(copies):
    for copy in copies:
        copy.start()


def wait_all(copies):
    for copy in copies:
        copy.wait()


def near_kernel(
    inv2_ref, rows_a, rows_b, base_a, base_b, face_b, fold_ref, out_a, out_b, left_c, left_d
):
    side = face_b.shape[0]
    right = parts_of(rows_a[...])
    scaled = mul_parts(right, parts_of(inv2_ref[...]), ((0,), (0,)))
    left_c[:, side:] = -scaled[:, :side]
    left_d[:, side:] = -scaled[:, side:]
    scaled = parts_of(scaled)
    mixed = mul_parts(scaled, parts_of(fold_ref[...]))
    left_c[:, :side] = mixed
    left_d[:, :side] = mixed
    out_a[...] = base_a[...] - mul_parts(scaled, right)
    sib = rows_b[...]
    sib = jnp.concatenate([sib[:side], sib[side:] + face_b[...]], axis=0)
    out_b[...] = base_b[...] - mul_parts(scaled, parts_of(sib))


def cross_kernel(
    place_ref, fold_any, shift_any, out_a, out_b, left_c, left_d, two_c, three_c, four_c, two_d, three_d,
    inv2_ref, total_ref, out_any, part_d, map_ref, base_ref, out_c, fold, shift, sems,
):
    width = two_c.shape[1]
    side = width // 2
    stores = [
        pltpu.make_async_copy(ref, out_any.at[:, lanes_of(place_ref, k, width)], sems.at[k])
        for k, ref in enumerate((out_a, out_b, out_c))
    ]
    loads = [
        pltpu.make_async_copy(fold_any, fold, sems.at[3]),
        pltpu.make_async_copy(shift_any, shift, sems.at[4]),
    ]
    start_all(loads)
    start_all(stores[:2])
    out_c[...] = mul(left_c[...], jnp.concatenate([two_c[...], three_c[...], four_c[...]], axis=0))
    stores[2].start()
    far_d = jnp.concatenate([two_d[...], three_d[...]], axis=0)
    part_d[...] = mul(left_d[:, : far_d.shape[0]], far_d)
    wait_all(loads)
    upper = -inv2_ref[:side]
    lower = mul_t(fold[...], inv2_ref[...])
    map_ref[:side] = upper[:, side:]
    map_ref[side:] = lower[:, side:]
    total = parts_of(total_ref[...])
    base_ref[:side] = mul_parts(parts_of(upper[:, :side]), total)
    base_ref[side:] = mul_parts(parts_of(lower[:, :side]), total) + shift[...]
    wait_all(stores)


def last_kernel(
    place_ref, in_any, part_d, left_d, four_d, map_ref, base_ref, total_ref,
    out_any, values_any, out_d, values, sems,
):
    tail, width = four_d.shape
    right = parts_of(four_d[...])
    values[...] = base_ref[...] + mul(map_ref[...], total_ref[...])
    values_store = pltpu.make_async_copy(values, values_any, sems.at[4])
    values_store.start()
    stores = pieces(out_d, out_any, sems, 0, lanes_of(place_ref, 3, width))
    rows = width // len(stores)
    for k, store in enumerate(stores):
        part = slice(k * rows, (k + 1) * rows)
        out_d[part] = part_d[part] + mul_parts(parts_of(left_d[part, width - tail :]), right)
        store.start()
    wait_all(stores + [values_store])


COSTS = {'*': 1000000000, 'own_level': 1500000000, 'own_term': 300000000, 'far_level': 1800000000, 'face_start': 1800000000, 'face_end': 1200000000}


def call(kernel, outs, args, us, name, specs=None, out_specs=None, scratch=(), aliases=None):
    return pl.pallas_call(
        kernel,
        out_shape=[
            pltpu.HBM(s, f32) if spec is HBM else jax.ShapeDtypeStruct(s, f32)
            for s, spec in zip(outs, out_specs or [VM] * len(outs))
        ],
        in_specs=specs or [VM] * len(args),
        out_specs=out_specs or [VM] * len(outs),
        scratch_shapes=[pltpu.VMEM(s, f32) if isinstance(s, tuple) else s for s in scratch],
        compiler_params=pltpu.CompilerParams(vmem_limit_bytes=12 * 1024 * 1024),
        cost_estimate=pl.CostEstimate(flops=COSTS.get(name, COSTS["*"]), bytes_accessed=0, transcendentals=0),
        input_output_aliases=aliases or {},
        name=name,
    )(*args)


def in_hbm(array):
    return pltpu.with_memory_space_constraint(array, pltpu.HBM)


def after(arrays, done):
    return lax.optimization_barrier((*arrays, done))


def body(leaf_raw, medium_class, wave_table, boundary_data):
    raw = leaf_raw[0, 0]
    classes = medium_class[0, 0]
    data = boundary_data[0, 0]
    bound = raw.shape[0]
    side = bound // 4
    ncol = data.shape[1]
    half_x = lax.axis_size("gx") // 2
    half_y = lax.axis_size("gy") // 2
    column = lax.axis_index("gx") // half_x
    row = lax.axis_index("gy") // half_y
    place = jnp.stack(
        [2 * row + column, 2 * row + 1 - column, 2 - 2 * row + column, 3 - 2 * row - column]
    ).astype(jnp.int32)
    sq, sq2, wide, thin = (side, side), (2 * side, 2 * side), (side, 2 * side), (2 * side, side)
    narrow = (side, ncol)

    third = 2 * side // 3
    full = (2 * side, 8 * side)
    (one,) = call(
        pack_kernel,
        [(side + 8, 2 * side)],
        tuple(in_hbm(x) for x in (classes, wave_table, raw)),
        1,
        "pack",
        specs=[HBM] * 3,
        scratch=[
            pltpu.SMEM(classes.shape, jnp.int32),
            pltpu.SMEM(wave_table.shape, f32),
            sq2,
            pltpu.SemaphoreType.DMA((3,)),
        ],
    )
    two, three, four, face, more = call(
        outer_kernel,
        [(third, 2 * side)] * 3 + [wide, (side + ncol // 2, 2 * side)],
        tuple(in_hbm(x) for x in (raw, data)),
        1,
        "outer",
        specs=[HBM] * 2,
        scratch=[sq2, data.shape, pltpu.SemaphoreType.DMA((2,))],
    )
    one_z = shifted(one, "gy")
    one_x = shifted(one, "gx")
    more_s, one_x = after((more,), one_x)
    more_x = shifted(more_s, "gx")
    inv1, fold1, face1 = call(
        own_kernel, [sq, thin, sq2], (one, one_x), 5, "own_level", scratch=[sq]
    )
    two_s, one_z, inv1 = after((two, one_z), inv1)
    two_z = shifted(two_s, "gy")
    one_zx = shifted(one_z, "gx")
    term, known = call(
        term_kernel, [narrow] * 2, (fold1, more, more_x, face, data), 1, "own_term"
    )
    three_s, more_x, term = after((three, more_x), term)
    three_z = shifted(three_s, "gy")
    rows_a, rows_b, base_a, base_b, fold_h, shift = call(
        rows_kernel,
        [sq2] * 4 + [thin, narrow],
        (in_hbm(raw), one, fold1, inv1, more, more_x, face, known),
        2,
        "pair_rows",
        specs=[HBM] + [VM] * 7,
        out_specs=[VM] * 4 + [HBM] * 2,
        scratch=[sq2, narrow, pltpu.SemaphoreType.DMA((3,))],
    )
    one_zx, rows_a = after((one_zx,), rows_a)
    face_s, one_zx = after((face,), one_zx)
    face_x = shifted(face_s, "gx")
    fold2, sum2 = call(
        far_kernel, [thin, sq2], (one_z, one_zx, face1), 6, "far_level", scratch=[sq, sq]
    )
    start2, bound2 = call(
        face_start_kernel, [sq2, (8, 128)], (one, sum2), 6, "face_start", scratch=[sq2]
    )
    two_z, start2 = after((two_z,), start2)
    two_zx = shifted(two_z, "gx")
    start2, two_z = after((start2,), two_z)
    four_s, term_s, start2 = after((four, term), start2)
    four_z = shifted(four_s, "gy")
    term_z = shifted(term_s, "gy")
    three_z, start2 = after((three_z,), start2)
    three_zx = shifted(three_z, "gx")
    start2, three_z = after((start2,), three_z)
    (inv2,) = call(face_end_kernel, [sq2], (sum2, start2, bound2), 4, "face_end")
    out_a, out_b, left_c, left_d = call(
        near_kernel,
        [sq2] * 4,
        (inv2, rows_a, rows_b, base_a, base_b, face_x, fold2),
        3,
        "near_rows",
    )
    term_z, left_c = after((term_z,), left_c)
    total = term + term_z
    total_x = shifted(total, "gx")
    four_z, total = after((four_z,), total)
    four_zx = shifted(four_z, "gx")
    parent, part_d, value_map, value_base = call(
        cross_kernel,
        [full, sq2, thin, (2 * side, ncol)],
        (
            place, in_hbm(fold_h), in_hbm(shift), out_a, out_b, left_c, left_d, two_z, three_z, four_z,
            two_zx, three_zx, inv2, total,
        ),
        2,
        "cross_rows",
        specs=[SM, HBM, HBM] + [VM] * 11,
        out_specs=[HBM, VM, VM, VM],
        scratch=[sq2, thin, narrow, pltpu.SemaphoreType.DMA((5,))],
    )
    parent, values = call(
        last_kernel,
        [full, (2 * side, ncol)],
        (place, in_hbm(parent), part_d, left_d, four_zx, value_map, value_base, total_x),
        2,
        "last_rows",
        specs=[SM, HBM] + [VM] * 6,
        out_specs=[HBM, HBM],
        scratch=[sq2, (2 * side, ncol), pltpu.SemaphoreType.DMA((5,))],
        aliases={1: 0},
    )
    return (parent[None, None], values[None, None])


def solution(mesh):
    return jax.shard_map(
        body,
        mesh=mesh,
        in_specs=(P("gx", "gy", None, None), P("gx", "gy", None), P(), P("gx", "gy", None, None)),
        out_specs=(P("gx", "gy", None, None), P("gx", "gy", None, None)),
        check_vma=False,
    )
```
